512 devices in a mesh: ctx: 32 (over x, y, core), row: 16 (over z).
Axes of the slice: x: 4, y: 4, z: 16, core: 2. Of those that a mesh axis runs over, the one named last changes fastest.
Arguments:
- queries: bfloat16 [64, 8192], P('row'), may hold values from -100 to 100
- shared_prefix_cache: bfloat16 [2, 131072, 1024], P(None, ('ctx', 'row')), may hold values from -6 to 6
- row_suffix_cache: bfloat16 [2, 64, 1024, 1024], P(None, 'row', 'ctx'), may hold values from -9 to 9
- row_suffix_length: int32 [64], P('row'), may hold values from 1 to 1024, as said below
- row_adapter_index: int32 [64, 1], P('row'), may hold values from 0 to 15; in each aligned block of 4 rows (0 to 3, 4 to 7, ...) at most 2 rows name the same one
- adapter_down_factor: bfloat16 [16, 8192, 16], P('row', 'ctx'), may hold values from -0.0625 to 0.0625
- adapter_up_factor: bfloat16 [16, 16, 8192], P('row', None, 'ctx'), may hold values from -1.5 to 1.5
Outputs:
- attended: bfloat16 [64, 8192], P('row', 'ctx')
- mixed: bfloat16 [64, 8192], P('row', 'ctx')
The draws below stay inside these ranges and needn't reach their ends.
Inputs may be any that keep to these rules, and one draw needn't show every extreme that they name: `row_suffix_length`: some row has exactly 1024 live suffix positions. `row_adapter_index`: among the 4 rows of one index of row (aligned blocks of rows), no adapter is named by more than 2 rows; some adapter is named by exactly 2 rows of a block.
All inputs are finite; a program needn't handle non-finite values.
Results may differ from the reference program's by a relative error of at most 0.006.
Values may be sent and summed in bfloat16 or wider, within the bound.
A program may use at most 64 MiB of HBM per device.

```python
import math
import jax
import jax.numpy as jnp
import numpy as np
from jax import lax

HEADS = 64
KV = 8
HD = 128
QUERY_FEATURES = 8192
ADAPTER_RANK = 16
ADAPTER_COUNT = 16
ROWS_DEV = 4
CAP = 2
ROWS = 64
PREF_DEV = 256
PREFIX = 131072
SUF = 1024


def draw_queries(key, part):
    key = jax.random.fold_in(key, 11)
    base_key = jax.random.fold_in(key, 0)
    return jnp.clip(jax.random.normal(base_key, (ROWS, QUERY_FEATURES), jnp.float32) * 3.0, -18.0, 18.0).astype(jnp.bfloat16)


def draw_row_suffix_length(key, part):
    key = jax.random.fold_in(key, 23)
    first, second = jax.random.split(key)
    lengths = jax.random.randint(first, (ROWS,), 1, SUF + 1)
    longest = jax.random.randint(second, (), 0, ROWS)
    return jnp.where(jnp.arange(ROWS) == longest, SUF, lengths).astype(jnp.int32)


def shard_levels(own_key, extent, cuts, low, high):
    factor_of = 1.0
    for axis_at, parts in cuts:
        heights = jax.random.uniform(jax.random.fold_in(jax.random.fold_in(own_key, 6), axis_at), (parts,), jnp.float32, low / len(cuts), high / len(cuts))
        factor_of = factor_of * jnp.repeat(jnp.exp(heights), extent[axis_at] // parts).reshape((-1,) + (1,) * (len(extent) - 1 - axis_at))
    return factor_of


def shared_out(stream_key, own, number, rows, amount, top, bound, slope):
    sequence = jax.random.permutation(stream_key, amount)
    crowded, usual = portions_of(amount, rows * top, bound, slope, True), portions_of(amount, rows * top, bound, slope, False)
    places = jnp.arange(amount)

    def named(tallies, turn):
        used = int((tallies > 0).sum())
        fixed = max(1, used // 4)
        passed = fixed + (places - fixed + turn * (used - fixed)) % max(1, amount - fixed)
        return jnp.zeros((amount,), jnp.int32).at[sequence[jnp.where(places < fixed, places, passed)]].set(jnp.asarray(tallies, jnp.int32))

    tallies = jnp.where(number % 4 == 0, named(crowded, number // 4), named(usual, number - number // 4 - 1))
    mixed = jax.random.permutation(jax.random.fold_in(own, 3), amount)
    giver, sink = mixed[0:amount // 2 * 2:2], mixed[1:amount // 2 * 2:2]
    margin = jnp.minimum(tallies[giver] - 1, bound - tallies[sink]) // 2
    margin = jnp.where((giver == sequence[0]) | (sink == sequence[0]) | (tallies[sink] == 0), 0, jnp.maximum(margin, 0))
    passed = jax.random.randint(jax.random.fold_in(own, 4), (amount // 2,), 0, 1 << 20) % (margin + 1)
    tallies = tallies.at[giver].add(-passed).at[sink].add(passed)
    items = jnp.searchsorted(jnp.cumsum(tallies), jnp.arange(rows * top), side="right").astype(jnp.int32)
    listing = items.reshape(top, rows).T
    listing = listing[jax.random.permutation(jax.random.fold_in(own, 1), rows)]
    turn = jax.random.randint(jax.random.fold_in(own, 2), (rows, 1), 0, top)
    return jnp.take_along_axis(listing, (jnp.arange(top)[None, :] + turn) % top, axis=1)


def portions_of(count, total, limit, slope, full):
    portions = [(1 << 20) // math.isqrt(standing ** slope) + 1 for standing in range(1, count + 1)]
    largest = limit if full else min(limit, max(-(-total // count), total * portions[0] // sum(portions)))
    least = 1 if total - largest >= count - 1 else 0
    given, spare = [largest] + [least] * (count - 1), total - largest - least * (count - 1)
    while spare > 0:
        movable = [i for i in range(1, count) if given[i] < largest] or [i for i in range(1, count) if given[i] < limit]
        mass, left = sum([portions[i] for i in movable]), spare
        for i in movable:
            extra = min(limit - given[i], max(1, left * portions[i] // mass), spare)
            given[i] = given[i] + extra
            spare = spare - extra
    return np.array(given)


def centred(stream_key, dims, width, reach, shards=(), kind=jnp.bfloat16):
    values = jax.random.normal(stream_key, dims, jnp.float32) * width
    if len(shards) > 0:
        values = shard_levels(stream_key, dims, shards, -0.22, 0.18) * values
    return jnp.clip(values, min=-reach, max=reach).astype(kind)


def setup_inputs(seed: int = 0) -> dict:
    splits = jax.random.split(jax.random.key(seed), 8)
    queries = draw_queries(jax.random.fold_in(splits[7], 71), 0)
    shared_prefix_cache = centred(splits[1], (2, PREFIX, KV * HD), 1.0, 6.0, ((1, 512),))
    row_suffix_cache = centred(splits[2], (2, ROWS, SUF, KV * HD), 1.5, 9.0, ((1, 16), (2, 32)))
    row_suffix_length = draw_row_suffix_length(jax.random.fold_in(splits[7], 71), 0)
    row_adapter_index_keys = jax.random.split(jax.random.fold_in(splits[4], 1), ROWS // ROWS_DEV)
    row_adapter_index_turns = jax.random.permutation(jax.random.fold_in(splits[4], 3), ROWS // ROWS_DEV)
    row_adapter_index = jax.vmap(lambda own, number: shared_out(jax.random.fold_in(splits[4], 2), own, number, ROWS_DEV, ADAPTER_COUNT, 1, CAP, 2))(row_adapter_index_keys, row_adapter_index_turns).reshape((ROWS, 1))
    adapter_down_factor = centred(splits[5], (ADAPTER_COUNT, QUERY_FEATURES, ADAPTER_RANK), QUERY_FEATURES ** -0.5, 0.0625, ((0, 16), (1, 32)))
    adapter_up_factor = centred(splits[6], (ADAPTER_COUNT, ADAPTER_RANK, QUERY_FEATURES), ADAPTER_RANK ** -0.5, 1.5, ((0, 16), (2, 32)))
    return dict(queries=queries, shared_prefix_cache=shared_prefix_cache, row_suffix_cache=row_suffix_cache, row_suffix_length=row_suffix_length, row_adapter_index=row_adapter_index, adapter_down_factor=adapter_down_factor, adapter_up_factor=adapter_up_factor)


def reference(queries, shared_prefix_cache, row_suffix_cache, row_suffix_length, row_adapter_index, adapter_down_factor, adapter_up_factor):
    rows = queries.shape[0]
    group = HEADS // KV
    scale = HD ** -0.5
    query_heads = queries.astype(jnp.float32).reshape(rows, KV, group, HD)
    blocks = PREFIX // PREF_DEV
    keys = shared_prefix_cache[0].reshape(blocks, PREF_DEV, KV, HD)
    values = shared_prefix_cache[1].reshape(blocks, PREF_DEV, KV, HD)

    def block_scores(key_block):
        return jnp.einsum('rgjd,kgd->rgjk', query_heads, key_block.astype(jnp.float32)) * scale

    suf_keys = row_suffix_cache[0].astype(jnp.float32).reshape(rows, SUF, KV, HD)
    suf_values = row_suffix_cache[1].astype(jnp.float32).reshape(rows, SUF, KV, HD)
    valid = (jnp.arange(SUF, dtype=jnp.int32)[None, :] < row_suffix_length[:, None])[:, None, None, :]
    suf_scores = jnp.where(valid, jnp.einsum('rgjd,rkgd->rgjk', query_heads, suf_keys) * scale, -1e30)

    def max_step(top, key_block):
        return jnp.maximum(top, block_scores(key_block).max(-1)), None

    top, unused = lax.scan(max_step, suf_scores.max(-1), keys)

    def sum_step(carry, pair):
        total, acc = carry
        key_block, value_block = pair
        weights = jnp.exp(block_scores(key_block) - top[..., None])
        rounded = lax.optimization_barrier(weights.astype(jnp.bfloat16)).astype(jnp.float32)
        acc = acc + jnp.einsum('rgjk,kgd->rgjd', rounded, value_block.astype(jnp.float32))
        return (total + weights.sum(-1), acc), None

    suf_weights = jnp.where(valid, jnp.exp(suf_scores - top[..., None]), 0.0)
    suf_rounded = lax.optimization_barrier(suf_weights.astype(jnp.bfloat16)).astype(jnp.float32)
    start = (suf_weights.sum(-1), jnp.einsum('rgjk,rkgd->rgjd', suf_rounded, suf_values))
    (total, acc), unused = lax.scan(sum_step, start, (keys, values))
    attended = (acc / total[..., None]).reshape(rows, HEADS * HD).astype(jnp.bfloat16)

    expert_index = row_adapter_index[:, 0].astype(jnp.int32)
    wide = lax.optimization_barrier(attended).astype(jnp.float32)
    down_factor_rows = jnp.take(adapter_down_factor, expert_index, axis=0).astype(jnp.float32)
    low = jnp.einsum('rf,rfk->rk', wide, down_factor_rows)
    low_rounded = lax.optimization_barrier(low.astype(jnp.bfloat16)).astype(jnp.float32)
    up_factor_rows = jnp.take(adapter_up_factor, expert_index, axis=0).astype(jnp.float32)
    delta = jnp.einsum('rk,rkf->rf', low_rounded, up_factor_rows).astype(jnp.bfloat16)
    mixed = (wide + lax.optimization_barrier(delta).astype(jnp.float32)).astype(jnp.bfloat16)
    return attended, mixed
```

```python
import functools
import math

import jax
import jax.numpy as jnp
from jax import lax
from jax.experimental import pallas as pl
from jax.experimental.pallas import tpu as pltpu
from jax.sharding import PartitionSpec as P

HD = 128
GROUP = 8
OWN = 4
VEC = 16
EXTRA = 16
MESH = pl.DeviceIdType.MESH
F32 = jnp.float32
BF16 = jnp.bfloat16


def three(value):
    high = value.astype(BF16).astype(F32)
    rest = value - high
    middle = rest.astype(BF16).astype(F32)
    return [high, middle, rest - middle]


def stacked(rows, count):
    width = rows[0].shape[1]
    at = lax.broadcasted_iota(jnp.int32, (count, width), 0)
    out = jnp.zeros((count, width), F32)
    for index, row in enumerate(rows):
        out = jnp.where(at == index, jnp.broadcast_to(row, (count, width)), out)
    return out


def contract_last(a, b):
    return lax.dot_general(a, b, (((1,), (1,)), ((), ())), preferred_element_type=F32)


def kernel(
    n_ctx,
    n_row,
    q_hbm,
    kv_hbm,
    suf_hbm,
    len_ref,
    idx_ref,
    down_hbm,
    up_hbm,
    att_ref,
    mix_ref,
    qv,
    q32,
    qown,
    kvs,
    vt,
    bias,
    qbuf,
    obuf,
    rbuf,
    zs,
    zr,
    ad,
    ls,
    lr,
    s_q,
    s_loc,
    s_sib_send,
    s_sib_recv,
    s_ad_loc,
    s_ad_send,
    s_ad_recv,
    s_a1_send,
    s_a1_recv,
    s_a2_send,
    s_a2_recv,
    s_o_send,
    s_o_recv,
    s_z_send,
    s_z_recv,
    s_l_send,
    s_l_recv,
):
    chips = n_ctx // 2
    pairs = chips // 2
    half = n_row // 2
    lanes = half * VEC
    pd = kv_hbm.shape[1]
    sd = suf_hbm.shape[1]
    spos = sd // OWN
    scale = HD**-0.5 * math.log2(math.e)

    ctx = lax.axis_index("ctx")
    z = lax.axis_index("row")
    c = lax.rem(ctx, 2)
    chip = ctx // 2
    g0 = chip // 2
    yl = lax.rem(chip, 2)
    zi = z // 2
    zp = lax.rem(z, 2)
    ablk = lax.rem(z + yl, 2)
    blk = g0 * 2 + ablk
    sib = ctx + 1 - 2 * c
    mate = ctx + 2 - 4 * yl

    q_copy = pltpu.make_async_copy(q_hbm, qv, s_q)
    q_copy.start()
    loc = []
    for i in range(2):
        loc.append(pltpu.make_async_copy(kv_hbm.at[i], kvs.at[i, 0:pd], s_loc.at[2 * i]))
        loc.append(
            pltpu.make_async_copy(
                suf_hbm.at[i], kvs.at[i, 2 * pd : 2 * pd + sd], s_loc.at[2 * i + 1]
            )
        )
    for copy in loc:
        copy.start()
    ad_loc = [
        pltpu.make_async_copy(down_hbm.at[0], ad.at[z, 0], s_ad_loc.at[0]),
        pltpu.make_async_copy(up_hbm.at[0], ad.at[z, 1], s_ad_loc.at[1]),
    ]
    for copy in ad_loc:
        copy.start()

    barrier = pltpu.get_barrier_semaphore()

    def greet_plane(d, carry):
        pl.semaphore_signal(
            barrier, 1, device_id=(lax.rem(ctx + d, n_ctx), z), device_id_type=MESH
        )
        return carry

    def greet_line(d, carry):
        pl.semaphore_signal(
            barrier, 1, device_id=(ctx, lax.rem(z + d, n_row)), device_id_type=MESH
        )
        return carry

    def greet_mate(i, carry):
        pl.semaphore_signal(
            barrier,
            1,
            device_id=(mate, lax.rem(z + 2 * i + 1 - yl, n_row)),
            device_id_type=MESH,
        )
        return carry

    lax.fori_loop(1, n_ctx, greet_plane, 0)
    lax.fori_loop(1, n_row, greet_line, 0)
    lax.fori_loop(yl, half, greet_mate, 0)

    q_copy.wait()
    for hh in range(4):
        head = g0 * GROUP + 4 * (hh // 2) + 2 * c + hh % 2
        start = pl.multiple_of(head * HD, HD)
        q32[hh * OWN : (hh + 1) * OWN, :] = qv[:, pl.ds(start, HD)].astype(F32)
    qown[...] = q32[...].astype(BF16)

    pl.semaphore_wait(barrier, n_ctx - 1 + n_row - 1 + half - 1 + yl)

    slot = g0 * 2 + zp
    place = pl.ds(pl.multiple_of(zi * VEC, VEC), VEC)

    def send_a1(i, carry):
        target = 2 * lax.rem(zi + i, half) + ablk
        pltpu.make_async_remote_copy(
            src_ref=qown,
            dst_ref=qbuf.at[slot, place],
            send_sem=s_a1_send,
            recv_sem=s_a1_recv,
            device_id=(ctx, target),
            device_id_type=MESH,
        ).start()
        return carry

    lax.fori_loop(1 - yl, half, send_a1, 0)

    @pl.when(yl == 0)
    def _():
        pltpu.make_async_copy(qown, qbuf.at[slot, place], s_a1_recv).start()

    sibling = []
    for i in range(2):
        sibling.append(
            pltpu.make_async_remote_copy(
                src_ref=kv_hbm.at[i],
                dst_ref=kvs.at[i, pd : 2 * pd],
                send_sem=s_sib_send.at[2 * i],
                recv_sem=s_sib_recv.at[2 * i],
                device_id=(sib, z),
                device_id_type=MESH,
            )
        )
        sibling.append(
            pltpu.make_async_remote_copy(
                src_ref=suf_hbm.at[i],
                dst_ref=kvs.at[i, 2 * pd + sd : 2 * pd + 2 * sd],
                send_sem=s_sib_send.at[2 * i + 1],
                recv_sem=s_sib_recv.at[2 * i + 1],
                device_id=(sib, z),
                device_id_type=MESH,
            )
        )
    for copy in sibling:
        copy.start()

    at = lax.broadcasted_iota(jnp.int32, (2 * sd, lanes), 0)
    lane = lax.broadcasted_iota(jnp.int32, (2 * sd, lanes), 1)
    owner = lax.rem(at, sd) // spos
    holder = jnp.where(at < sd, ctx, sib)
    position = holder * spos + lax.rem(at, spos)
    live = jnp.zeros((2 * sd, lanes), jnp.int32)
    for k in range(OWN):
        live = jnp.where(owner == k, len_ref[k], live)
    valid = (lane // VEC == zi) & (lax.rem(lane, OWN) == owner) & (position < live)
    bias[...] = jnp.where(valid, 0.0, -1e30).astype(F32)

    pltpu.make_async_copy(qbuf.at[blk], qbuf.at[blk], s_a1_recv).wait()

    def send_a2(i, carry):
        target = lax.rem(g0 + pairs - i // 2, pairs) * 2 + lax.rem(yl + i, 2)
        pltpu.make_async_remote_copy(
            src_ref=qbuf.at[blk],
            dst_ref=qbuf.at[blk],
            send_sem=s_a2_send,
            recv_sem=s_a2_recv.at[blk],
            device_id=(target * 2 + c, z),
            device_id_type=MESH,
        ).start()
        return carry

    lax.fori_loop(1, chips, send_a2, 0)

    for copy in ad_loc:
        copy.wait()

    def send_ad(d, carry):
        pltpu.make_async_remote_copy(
            src_ref=ad.at[z],
            dst_ref=ad.at[z],
            send_sem=s_ad_send,
            recv_sem=s_ad_recv,
            device_id=(ctx, lax.rem(z + d, n_row)),
            device_id_type=MESH,
        ).start()
        return carry

    lax.fori_loop(1, n_row, send_ad, 0)

    for copy in loc:
        copy.wait()
    for copy in sibling:
        copy.wait()

    def turn_values(g, carry):
        columns = pl.ds(pl.multiple_of(g * HD, HD), HD)
        vt[g] = kvs[1, :, columns].T
        return carry

    lax.fori_loop(0, pairs, turn_values, 0)

    def attend(t, carry):
        g = lax.rem(g0 + t, pairs)
        for a in range(2):

            @pl.when(2 * g + a != blk)
            def _():
                pltpu.make_async_copy(
                    qbuf.at[2 * g + a], qbuf.at[2 * g + a], s_a2_recv.at[2 * g + a]
                ).wait()

        columns = pl.ds(pl.multiple_of(g * HD, HD), HD)
        sides = (zp, 1 - zp)
        near = qbuf[2 * g + zp]
        both = jnp.concatenate([near, qbuf[2 * g + 1 - zp]], axis=0)
        scores = contract_last(kvs[0, 0 : 2 * pd, columns], both) * scale
        suffix = contract_last(kvs[0, 2 * pd : 2 * pd + 2 * sd, columns], near) * scale
        suffix = suffix + bias[...]
        top = jnp.max(scores, axis=0, keepdims=True)
        top_near = jnp.maximum(top[:, :lanes], jnp.max(suffix, axis=0, keepdims=True))
        top = jnp.concatenate([top_near, top[:, lanes:]], axis=1)
        weights = jnp.exp2(scores - top)
        weights_near = jnp.exp2(suffix - top_near)
        total = jnp.sum(weights, axis=0, keepdims=True)
        total_near = jnp.sum(weights_near, axis=0, keepdims=True)
        acc = jnp.dot(
            vt[g, :, 0 : 2 * pd], weights.astype(BF16), preferred_element_type=F32
        )
        acc_near = jnp.dot(
            vt[g, :, 2 * pd : 2 * pd + 2 * sd],
            weights_near.astype(BF16),
            preferred_element_type=F32,
        )
        outs = (acc[:, :lanes] + acc_near, acc[:, lanes:])
        tops = (top_near, top[:, lanes:])
        totals = (total[:, :lanes] + total_near, total[:, lanes:])
        for j in range(2):
            index = 2 * g + sides[j]
            obuf[index, 0:HD, :] = outs[j].astype(BF16)
            obuf[index, HD : HD + EXTRA, :] = stacked(
                three(tops[j]) + three(totals[j]), EXTRA
            ).astype(BF16)
            target = 2 * g + lax.rem(sides[j] + z, 2)

            @pl.when(target != chip)
            def _():
                pltpu.make_async_remote_copy(
                    src_ref=obuf.at[index],
                    dst_ref=rbuf.at[chip],
                    send_sem=s_o_send,
                    recv_sem=s_o_recv,
                    device_id=(target * 2 + c, z),
                    device_id_type=MESH,
                ).start()

            @pl.when(target == chip)
            def _():
                pltpu.make_async_copy(obuf.at[index], rbuf.at[chip], s_o_recv).start()

        return carry

    lax.fori_loop(0, pairs, attend, 0)

    pltpu.make_async_copy(rbuf, rbuf, s_o_recv).wait()
    tops, totals = [], []
    for k in range(chips):
        extra = rbuf[k, HD : HD + EXTRA, :].astype(F32)
        tops.append(extra[0:1] + extra[1:2] + extra[2:3])
        totals.append(extra[3:4] + extra[4:5] + extra[5:6])
    top = functools.reduce(jnp.maximum, tops)
    acc = jnp.zeros((HD, lanes), F32)
    total = jnp.zeros((1, lanes), F32)
    for k in range(chips):
        factor = jnp.exp2(tops[k] - top)
        acc = acc + factor * rbuf[k, 0:HD, :].astype(F32)
        total = total + factor * totals[k]
    extra = stacked(three(top) + three(total), HD)
    zs[...] = jnp.concatenate(
        [acc.T.reshape(half, 2, 8, HD), extra.T.reshape(half, 2, 8, HD)], axis=2
    ).astype(BF16)

    def send_z(i, carry):
        at_z = lax.rem(zi + i, half)
        target_z = 2 * at_z + ablk
        for side in range(2):
            target = (g0 * 2 + side) * 2 + c
            here = (target == ctx) & (target_z == z)

            @pl.when(jnp.logical_not(here))
            def _():
                pltpu.make_async_remote_copy(
                    src_ref=zs.at[at_z, side],
                    dst_ref=zr.at[z],
                    send_sem=s_z_send,
                    recv_sem=s_z_recv,
                    device_id=(target, target_z),
                    device_id_type=MESH,
                ).start()

            @pl.when(here)
            def _():
                pltpu.make_async_copy(zs.at[at_z, side], zr.at[z], s_z_recv).start()

        return carry

    lax.fori_loop(0, half, send_z, 0)

    pltpu.make_async_copy(ad.at[0 : n_row - 1], ad.at[0 : n_row - 1], s_ad_recv).wait()

    pltpu.make_async_copy(zr, zr, s_z_recv).wait()
    arrived = zr[...].astype(F32)
    extra = arrived[:, 8:16, :].reshape(n_row * 8, HD).astype(BF16)
    row = lax.broadcasted_iota(jnp.int32, (HD, 2 * HD), 0)
    col = lax.broadcasted_iota(jnp.int32, (HD, 2 * HD), 1)
    pick = jnp.where(row // 3 == col // HD, 1.0, 0.0).astype(BF16)
    spread = jnp.dot(extra, pick, preferred_element_type=F32)
    tops = spread[:, :HD].reshape(n_row, 8, HD)
    totals = spread[:, HD:].reshape(n_row, 8, HD)
    factor = jnp.exp2(tops - jnp.max(tops, axis=0, keepdims=True))
    acc = jnp.sum(factor * arrived[:, 0:8, :], axis=0)
    total = jnp.sum(factor * totals, axis=0)
    attended = (acc / total).astype(BF16).astype(F32)
    attended = jnp.concatenate([attended[0:OWN], attended[OWN : 2 * OWN]], axis=1)
    att_ref[...] = attended.astype(BF16)

    rank = down_hbm.shape[1]
    width = n_row * rank // 2
    twice = jnp.concatenate([attended, attended], axis=0).astype(BF16)
    low = contract_last(twice, ad[:, 0].reshape(n_row * rank, 2 * HD))
    row = lax.broadcasted_iota(jnp.int32, (2 * OWN, width), 0)
    col = lax.broadcasted_iota(jnp.int32, (2 * OWN, width), 1)
    wanted = jnp.zeros((2 * OWN, width), jnp.int32)
    for k in range(OWN):
        wanted = jnp.where(lax.rem(row, OWN) == k, idx_ref[k, 0], wanted)
    mine = wanted == col // rank + (n_row // 2) * (row // OWN)
    low = jnp.where(row < OWN, low[:, :width], low[:, width:])
    ls[...] = jnp.where(mine, low, 0.0)
    lr[ctx] = ls[...]

    def send_l(d, carry):
        pltpu.make_async_remote_copy(
            src_ref=ls,
            dst_ref=lr.at[ctx],
            send_sem=s_l_send,
            recv_sem=s_l_recv,
            device_id=(lax.rem(ctx + d, n_ctx), z),
            device_id_type=MESH,
        ).start()
        return carry

    lax.fori_loop(1, n_ctx, send_l, 0)
    pltpu.make_async_copy(lr.at[0 : n_ctx - 1], lr.at[0 : n_ctx - 1], s_l_recv).wait()
    low = jnp.sum(lr[...], axis=0).astype(BF16)
    up = ad[:, 1].reshape(n_row * rank, 2 * HD)
    first = jnp.dot(low, up[:width], preferred_element_type=F32)
    second = jnp.dot(low, up[width:], preferred_element_type=F32)
    delta = first[0:OWN] + second[OWN : 2 * OWN]
    mix_ref[...] = (attended + delta.astype(BF16).astype(F32)).astype(BF16)

    @pl.when(yl == 0)
    def _():
        part = qbuf.at[0, 0 : lanes - VEC]
        pltpu.make_async_copy(part, part, s_a1_send).wait()
        part = zr.at[0 : n_row - 1]
        pltpu.make_async_copy(part, part, s_z_send).wait()

    @pl.when(yl == 1)
    def _():
        pltpu.make_async_copy(qbuf.at[0], qbuf.at[0], s_a1_send).wait()
        pltpu.make_async_copy(zr, zr, s_z_send).wait()

    part = qbuf.at[0 : chips - 1]
    pltpu.make_async_copy(part, part, s_a2_send).wait()
    part = obuf.at[0 : chips - 1]
    pltpu.make_async_copy(part, part, s_o_send).wait()
    part = ad.at[0 : n_row - 1]
    pltpu.make_async_copy(part, part, s_ad_send).wait()
    part = lr.at[0 : n_ctx - 1]
    pltpu.make_async_copy(part, part, s_l_send).wait()


def body(n_ctx, n_row, queries, prefix, suffix, lengths, adapters, down, up):
    chips = n_ctx // 2
    pairs = chips // 2
    half = n_row // 2
    lanes = half * VEC
    pd = prefix.shape[1]
    sd = suffix.shape[1] * suffix.shape[2]
    width = prefix.shape[2]
    rank = down.shape[2]
    suffix = suffix.reshape(2, sd, width)
    down = jnp.transpose(down, (0, 2, 1))
    hbm = pl.BlockSpec(memory_space=pl.ANY)
    smem = pl.BlockSpec(memory_space=pltpu.SMEM)
    vmem = pl.BlockSpec(memory_space=pltpu.VMEM)
    dma = pltpu.SemaphoreType.DMA
    out = jax.ShapeDtypeStruct((OWN, 2 * HD), BF16)
    return pl.pallas_call(
        functools.partial(kernel, n_ctx, n_row),
        out_shape=(out, out),
        in_specs=[hbm, hbm, hbm, smem, smem, hbm, hbm],
        out_specs=(vmem, vmem),
        scratch_shapes=[
            pltpu.VMEM(queries.shape, BF16),
            pltpu.VMEM((VEC, HD), F32),
            pltpu.VMEM((VEC, HD), BF16),
            pltpu.VMEM((2, 2 * pd + 2 * sd, width), BF16),
            pltpu.VMEM((pairs, HD, 2 * pd + 2 * sd), BF16),
            pltpu.VMEM((2 * sd, lanes), F32),
            pltpu.VMEM((chips, lanes, HD), BF16),
            pltpu.VMEM((chips, HD + EXTRA, lanes), BF16),
            pltpu.VMEM((chips, HD + EXTRA, lanes), BF16),
            pltpu.VMEM((half, 2, 16, HD), BF16),
            pltpu.VMEM((n_row, 16, HD), BF16),
            pltpu.VMEM((n_row, 2, rank, 2 * HD), BF16),
            pltpu.VMEM((2 * OWN, n_row * rank // 2), F32),
            pltpu.VMEM((n_ctx, 2 * OWN, n_row * rank // 2), F32),
            dma,
            dma((4,)),
            dma((4,)),
            dma((4,)),
            dma((2,)),
            dma,
            dma,
            dma,
            dma,
            dma,
            dma((chips,)),
            dma,
            dma,
            dma,
            dma,
            dma,
            dma,
        ],
        compiler_params=pltpu.CompilerParams(
            collective_id=0, has_side_effects=True, vmem_limit_bytes=40 * 1024 * 1024
        ),
        name="decode_attention",
    )(queries, prefix, suffix, lengths, adapters, down, up)


def solution(mesh):
    return jax.shard_map(
        functools.partial(body, mesh.shape["ctx"], mesh.shape["row"]),
        mesh=mesh,
        in_specs=(
            P("row", None),
            P(None, ("ctx", "row"), None),
            P(None, "row", "ctx", None),
            P("row"),
            P("row", None),
            P("row", "ctx", None),
            P("row", None, "ctx"),
        ),
        out_specs=(P("row", "ctx"), P("row", "ctx")),
        check_vma=False,
    )
```

```python
import functools
import math

import jax
import jax.numpy as jnp
from jax import lax
from jax.experimental import pallas as pl
from jax.experimental.pallas import tpu as pltpu
from jax.sharding import PartitionSpec as P

HD = 128
GROUP = 8
OWN = 4
VEC = 16
EXTRA = 16
COLUMN = 4
MESH = pl.DeviceIdType.MESH
F32 = jnp.float32
BF16 = jnp.bfloat16


def three(value):
    high = value.astype(BF16).astype(F32)
    rest = value - high
    middle = rest.astype(BF16).astype(F32)
    return [high, middle, rest - middle]


def stacked(parts, shape, axis):
    at = lax.broadcasted_iota(jnp.int32, shape, axis)
    out = jnp.zeros(shape, F32)
    for index, part in enumerate(parts):
        out = jnp.where(at == index, jnp.broadcast_to(part, shape), out)
    return out


def contract_last(a, b):
    return lax.dot_general(a, b, (((1,), (1,)), ((), ())), preferred_element_type=F32)


def merged(arrived):
    count = arrived.shape[0]
    wide = arrived.astype(F32)
    extra = wide[:, 8:16, :].reshape(count * 8, HD).astype(BF16)
    row = lax.broadcasted_iota(jnp.int32, (HD, 2 * HD), 0)
    col = lax.broadcasted_iota(jnp.int32, (HD, 2 * HD), 1)
    pick = jnp.where(row // 3 == col // HD, 1.0, 0.0).astype(BF16)
    spread = jnp.dot(extra, pick, preferred_element_type=F32)
    tops = spread[:, :HD].reshape(count, 8, HD)
    totals = spread[:, HD:].reshape(count, 8, HD)
    top = jnp.max(tops, axis=0)
    factor = jnp.exp2(tops - top[None])
    return top, jnp.sum(factor * totals, axis=0), jnp.sum(factor * wide[:, 0:8, :], axis=0)


def kernel(
    n_ctx,
    n_row,
    q_hbm,
    kv_hbm,
    suf_hbm,
    len_ref,
    idx_ref,
    down_hbm,
    up_hbm,
    att_ref,
    mix_ref,
    qv,
    qall,
    qown,
    sufv,
    sx,
    sr,
    kvb,
    vt,
    qb,
    sc,
    ob,
    rb,
    zs,
    zr,
    ad,
    ls,
    lr,
    s_q,
    s_suf,
    s_ad_loc,
    s_ad_send,
    s_ad_recv,
    s_a_send,
    s_a_recv,
    s_x_send,
    s_x_recv,
    s_kv_send,
    s_kv_recv,
    s_s_send,
    s_s_recv,
    s_o_send,
    s_o_recv,
    s_z_send,
    s_z_recv,
    s_l_send,
    s_l_recv,
):
    chips = n_ctx // 2
    pairs = chips // 2
    breadth = chips // COLUMN
    lanes = n_row * 8
    pd = kv_hbm.shape[1]
    sd = suf_hbm.shape[1]
    spos = sd // OWN
    scale = HD**-0.5 * math.log2(math.e)

    ctx = lax.axis_index("ctx")
    z = lax.axis_index("row")
    c = lax.rem(ctx, 2)
    chip = ctx // 2
    x = chip // COLUMN
    y = lax.rem(chip, COLUMN)
    g0 = chip // 2
    yl = lax.rem(chip, 2)
    sib = ctx + 1 - 2 * c

    q_copy = pltpu.make_async_copy(q_hbm, qv, s_q)
    q_copy.start()
    suf_copy = pltpu.make_async_copy(suf_hbm, sufv, s_suf)
    suf_copy.start()
    ad_loc = [
        pltpu.make_async_copy(down_hbm.at[0], ad.at[z, 0], s_ad_loc.at[0]),
        pltpu.make_async_copy(up_hbm.at[0], ad.at[z, 1], s_ad_loc.at[1]),
    ]
    for copy in ad_loc:
        copy.start()

    barrier = pltpu.get_barrier_semaphore()

    def greet_line(d, carry):
        pl.semaphore_signal(
            barrier, 1, device_id=(ctx, lax.rem(z + d, n_row)), device_id_type=MESH
        )
        return carry

    def greet_plane(d, carry):
        pl.semaphore_signal(
            barrier, 1, device_id=(lax.rem(ctx + d, n_ctx), z), device_id_type=MESH
        )
        return carry

    lax.fori_loop(1, n_row, greet_line, 0)
    lax.fori_loop(1, n_ctx, greet_plane, 0)

    q_copy.wait()
    queries = qv[...].astype(F32)
    for head in range(pairs * GROUP):
        qall[head * OWN : (head + 1) * OWN, :] = queries[:, head * HD : (head + 1) * HD]
    for side in range(2):
        start = pl.multiple_of(g0 * (GROUP * OWN) + side * VEC + 8 * c, 8)
        qown[side * 8 : (side + 1) * 8, :] = qall[pl.ds(start, 8), :]
    first = pl.ds(pl.multiple_of(z * VEC, VEC), VEC)
    qb[c, first, :] = qown[...].astype(BF16)

    pl.semaphore_wait(barrier, n_ctx - 1 + n_row - 1)

    def send_a(d, carry):
        pltpu.make_async_remote_copy(
            src_ref=qb.at[c, first],
            dst_ref=qb.at[c, first],
            send_sem=s_a_send,
            recv_sem=s_a_recv,
            device_id=(ctx, lax.rem(z + d, n_row)),
            device_id_type=MESH,
        ).start()
        return carry

    lax.fori_loop(1, n_row, send_a, 0)

    def place_kv(i, g):
        same = (g % 2) == y // 2
        target = (g // 2) * COLUMN + jnp.where(same, y, COLUMN - 1 - y)
        slot = 2 * x + jnp.where(same, 0, 1)
        columns = pl.ds(pl.multiple_of(g * HD, HD), HD)
        return target, slot, kv_hbm.at[i, :, columns]

    for i in range(2):

        def send_kv(d, carry):
            target, slot, part = place_kv(i, lax.rem(g0 + d, pairs))
            pltpu.make_async_remote_copy(
                src_ref=part,
                dst_ref=kvb.at[i, slot],
                send_sem=s_kv_send,
                recv_sem=s_kv_recv.at[i, slot],
                device_id=(target * 2 + c, z),
                device_id_type=MESH,
            ).start()
            return carry

        lax.fori_loop(1, pairs, send_kv, 0)
        _, slot, part = place_kv(i, g0)
        pltpu.make_async_copy(part, kvb.at[i, slot], s_kv_recv.at[i, slot]).start()

    for copy in ad_loc:
        copy.wait()

    def send_ad(d, carry):
        pltpu.make_async_remote_copy(
            src_ref=ad.at[z],
            dst_ref=ad.at[z],
            send_sem=s_ad_send,
            recv_sem=s_ad_recv,
            device_id=(ctx, lax.rem(z + d, n_row)),
            device_id_type=MESH,
        ).start()
        return carry

    lax.fori_loop(1, n_row, send_ad, 0)

    suf_copy.wait()
    at = lax.broadcasted_iota(jnp.int32, (GROUP * OWN, sd), 1)
    row = lax.broadcasted_iota(jnp.int32, (GROUP * OWN, sd), 0)
    owner = at // spos
    live = jnp.zeros((GROUP * OWN, sd), jnp.int32)
    for k in range(OWN):
        live = jnp.where(owner == k, len_ref[k], live)
    valid = (lax.rem(row, OWN) == owner) & (ctx * spos + lax.rem(at, spos) < live)
    for g in range(pairs):
        vectors = qall[g * GROUP * OWN : (g + 1) * GROUP * OWN, :].astype(BF16)
        scores = contract_last(vectors, sufv[0, :, g * HD : (g + 1) * HD]) * scale
        scores = jnp.where(valid, scores, -1e30)
        top = jnp.max(scores, axis=1, keepdims=True)
        weights = jnp.exp2(scores - top)
        total = jnp.sum(weights, axis=1, keepdims=True)
        out = jnp.dot(
            weights.astype(BF16),
            sufv[1, :, g * HD : (g + 1) * HD],
            preferred_element_type=F32,
        )
        extra = stacked(three(top) + three(total), (GROUP * OWN, HD), 1)
        sx[4 * g : 4 * g + 4] = jnp.concatenate(
            [out.reshape(4, 8, HD), extra.reshape(4, 8, HD)], axis=1
        ).astype(BF16)

    def send_s(d, carry):
        target = lax.rem(ctx + d, n_ctx)
        pltpu.make_async_remote_copy(
            src_ref=sx.at[target],
            dst_ref=sr.at[ctx],
            send_sem=s_s_send,
            recv_sem=s_s_recv,
            device_id=(target, z),
            device_id_type=MESH,
        ).start()
        return carry

    lax.fori_loop(1, n_ctx, send_s, 0)
    sr[ctx] = sx[ctx]

    def finish(k):
        part = ad.at[0 : n_row - 1]
        pltpu.make_async_copy(part, part, s_ad_send).wait()
        part = qb.at[0, 0 : (n_row - 1) * VEC]
        pltpu.make_async_copy(part, part, s_a_send).wait()
        part = kvb.at[:, 0 : pairs - 1]
        pltpu.make_async_copy(part, part, s_kv_send).wait()
        part = sx.at[0 : n_ctx - 1]
        pltpu.make_async_copy(part, part, s_s_send).wait()
        pltpu.make_async_copy(qb.at[0], qb.at[0], s_x_send).wait()
        part = ob.at[0:3]
        pltpu.make_async_copy(part, part, s_o_send).wait()
        part = zs.at[0 : n_row - 1]
        pltpu.make_async_copy(part, part, s_z_send).wait()
        part = lr.at[0 : n_ctx - 1]
        pltpu.make_async_copy(part, part, s_l_send).wait()

    part = qb.at[0, 0 : (n_row - 1) * VEC]
    pltpu.make_async_copy(part, part, s_a_recv).wait()
    exchange = pltpu.make_async_remote_copy(
        src_ref=qb.at[c],
        dst_ref=qb.at[c],
        send_sem=s_x_send,
        recv_sem=s_x_recv,
        device_id=(sib, z),
        device_id_type=MESH,
    )
    exchange.start()

    def vectors_of(core):
        wide = qb[core].astype(F32).reshape(n_row, 2, 8, HD)
        return jnp.concatenate(
            [wide[:, side].reshape(lanes, HD) for side in range(2)], axis=0
        ).astype(BF16)

    def chunk(j):
        return pl.multiple_of(2 * lax.rem(x + j, breadth), 2)

    def arrive(i, j):
        for side in range(2):
            slot = chunk(j) + side
            pltpu.make_async_copy(
                kvb.at[i, slot], kvb.at[i, slot], s_kv_recv.at[i, slot]
            ).wait()

    cores = (c, 1 - c)
    tops = []
    for h in range(2):
        if h == 1:
            exchange.wait_recv()
        vectors = vectors_of(cores[h])
        top = None
        for j in range(breadth):
            if h == 0:
                arrive(0, j)
            keys = kvb[0, pl.ds(chunk(j), 2)].reshape(2 * pd, HD)
            scores = contract_last(keys, vectors) * scale
            sc[h, j] = scores
            best = jnp.max(scores, axis=0, keepdims=True)
            top = best if top is None else jnp.maximum(top, best)
        tops.append(top)
    for j in range(breadth):
        arrive(1, j)
        vt[j] = kvb[1, pl.ds(chunk(j), 2)].reshape(2 * pd, HD).T

    for h in range(2):
        total = jnp.zeros((1, 2 * lanes), F32)
        acc = jnp.zeros((HD, 2 * lanes), F32)
        for j in range(breadth):
            weights = jnp.exp2(sc[h, j] - tops[h])
            total = total + jnp.sum(weights, axis=0, keepdims=True)
            acc = acc + jnp.dot(vt[j], weights.astype(BF16), preferred_element_type=F32)
        extra = stacked(three(tops[h]) + three(total), (EXTRA, 2 * lanes), 0)
        for side in range(2):
            target = (g0 * 2 + side) * 2 + cores[h]
            index = 2 * side + cores[h]
            columns = slice(side * lanes, (side + 1) * lanes)
            ob[index, 0:HD, :] = acc[:, columns].astype(BF16)
            ob[index, HD : HD + EXTRA, :] = extra[:, columns].astype(BF16)

            @pl.when(target != ctx)
            def _():
                pltpu.make_async_remote_copy(
                    src_ref=ob.at[index],
                    dst_ref=rb.at[2 * yl + c],
                    send_sem=s_o_send,
                    recv_sem=s_o_recv,
                    device_id=(target, z),
                    device_id_type=MESH,
                ).start()

            @pl.when(target == ctx)
            def _():
                pltpu.make_async_copy(ob.at[index], rb.at[2 * yl + c], s_o_recv).start()

    part = sr.at[0 : n_ctx - 1]
    pltpu.make_async_copy(part, part, s_s_recv).wait()
    near = merged(sr[...])

    pltpu.make_async_copy(rb, rb, s_o_recv).wait()
    tops, totals = [], []
    for k in range(4):
        extra = rb[k, HD : HD + EXTRA, :].astype(F32)
        tops.append(extra[0:1] + extra[1:2] + extra[2:3])
        totals.append(extra[3:4] + extra[4:5] + extra[5:6])
    top = functools.reduce(jnp.maximum, tops)
    acc = jnp.zeros((HD, lanes), F32)
    total = jnp.zeros((1, lanes), F32)
    for k in range(4):
        factor = jnp.exp2(tops[k] - top)
        acc = acc + factor * rb[k, 0:HD, :].astype(F32)
        total = total + factor * totals[k]
    extra = stacked(three(top) + three(total), (HD, lanes), 0)
    zs[...] = jnp.concatenate(
        [acc.T.reshape(n_row, 8, HD), extra.T.reshape(n_row, 8, HD)], axis=1
    ).astype(BF16)

    def send_z(d, carry):
        target = lax.rem(z + d, n_row)
        pltpu.make_async_remote_copy(
            src_ref=zs.at[target],
            dst_ref=zr.at[z],
            send_sem=s_z_send,
            recv_sem=s_z_recv,
            device_id=(ctx, target),
            device_id_type=MESH,
        ).start()
        return carry

    lax.fori_loop(1, n_row, send_z, 0)
    zr[z] = zs[z]

    pltpu.make_async_copy(ad.at[0 : n_row - 1], ad.at[0 : n_row - 1], s_ad_recv).wait()

    part = zr.at[0 : n_row - 1]
    pltpu.make_async_copy(part, part, s_z_recv).wait()
    far = merged(zr[...])
    top = jnp.maximum(near[0], far[0])
    parts = [jnp.exp2(near[0] - top), jnp.exp2(far[0] - top)]
    total = parts[0] * near[1] + parts[1] * far[1]
    acc = parts[0] * near[2] + parts[1] * far[2]
    attended = (acc / total).astype(BF16).astype(F32)
    attended = jnp.concatenate([attended[0:OWN], attended[OWN : 2 * OWN]], axis=1)
    att_ref[...] = attended.astype(BF16)

    rank = down_hbm.shape[1]
    width = n_row * rank // 2
    twice = jnp.concatenate([attended, attended], axis=0).astype(BF16)
    low = contract_last(twice, ad[:, 0].reshape(n_row * rank, 2 * HD))
    row = lax.broadcasted_iota(jnp.int32, (2 * OWN, width), 0)
    col = lax.broadcasted_iota(jnp.int32, (2 * OWN, width), 1)
    wanted = jnp.zeros((2 * OWN, width), jnp.int32)
    for k in range(OWN):
        wanted = jnp.where(lax.rem(row, OWN) == k, idx_ref[0, k], wanted)
    mine = wanted == col // rank + (n_row // 2) * (row // OWN)
    low = jnp.where(row < OWN, low[:, :width], low[:, width:])
    ls[...] = jnp.where(mine, low, 0.0)

    def send_l(d, carry):
        pltpu.make_async_remote_copy(
            src_ref=ls,
            dst_ref=lr.at[ctx],
            send_sem=s_l_send,
            recv_sem=s_l_recv,
            device_id=(lax.rem(ctx + d, n_ctx), z),
            device_id_type=MESH,
        ).start()
        return carry

    lax.fori_loop(1, n_ctx, send_l, 0)
    lr[ctx] = ls[...]
    pltpu.make_async_copy(lr.at[0 : n_ctx - 1], lr.at[0 : n_ctx - 1], s_l_recv).wait()
    low = jnp.sum(lr[...], axis=0).astype(BF16)
    up = ad[:, 1].reshape(n_row * rank, 2 * HD)
    first = jnp.dot(low, up[:width], preferred_element_type=F32)
    second = jnp.dot(low, up[width:], preferred_element_type=F32)
    delta = first[0:OWN] + second[OWN : 2 * OWN]
    mix_ref[...] = (attended + delta.astype(BF16).astype(F32)).astype(BF16)

    finish(99)


def body(n_ctx, n_row, queries, prefix, suffix, lengths, adapters, down, up):
    chips = n_ctx // 2
    pairs = chips // 2
    breadth = chips // COLUMN
    lanes = n_row * 8
    pd = prefix.shape[1]
    sd = suffix.shape[1] * suffix.shape[2]
    width = prefix.shape[2]
    rank = down.shape[2]
    suffix = suffix.reshape(2, sd, width)
    adapters = adapters.T
    down = jnp.transpose(down, (0, 2, 1))
    hbm = pl.BlockSpec(memory_space=pltpu.HBM)
    smem = pl.BlockSpec(memory_space=pltpu.SMEM)
    vmem = pl.BlockSpec(memory_space=pltpu.VMEM)
    dma = pltpu.SemaphoreType.DMA
    out = jax.ShapeDtypeStruct((OWN, 2 * HD), BF16)
    return pl.pallas_call(
        functools.partial(kernel, n_ctx, n_row),
        out_shape=(out, out),
        in_specs=[hbm, hbm, hbm, smem, smem, hbm, hbm],
        out_specs=(vmem, vmem),
        scratch_shapes=[
            pltpu.VMEM(queries.shape, BF16),
            pltpu.VMEM((pairs * GROUP * OWN, HD), F32),
            pltpu.VMEM((VEC, HD), F32),
            pltpu.VMEM(suffix.shape, BF16),
            pltpu.VMEM((n_ctx, 16, HD), BF16),
            pltpu.VMEM((n_ctx, 16, HD), BF16),
            pltpu.VMEM((2, 2 * breadth, pd, HD), BF16),
            pltpu.VMEM((breadth, HD, 2 * pd), BF16),
            pltpu.VMEM((2, n_row * VEC, HD), BF16),
            pltpu.VMEM((2, breadth, 2 * pd, 2 * lanes), F32),
            pltpu.VMEM((4, HD + EXTRA, lanes), BF16),
            pltpu.VMEM((4, HD + EXTRA, lanes), BF16),
            pltpu.VMEM((n_row, 16, HD), BF16),
            pltpu.VMEM((n_row, 16, HD), BF16),
            pltpu.VMEM((n_row, 2, rank, 2 * HD), BF16),
            pltpu.VMEM((2 * OWN, n_row * rank // 2), F32),
            pltpu.VMEM((n_ctx, 2 * OWN, n_row * rank // 2), F32),
            dma,
            dma,
            dma((2,)),
            dma,
            dma,
            dma,
            dma,
            dma,
            dma,
            dma,
            dma((2, 2 * breadth)),
            dma,
            dma,
            dma,
            dma,
            dma,
            dma,
            dma,
            dma,
        ],
        compiler_params=pltpu.CompilerParams(
            collective_id=0, has_side_effects=True, vmem_limit_bytes=64 * 1024 * 1024
        ),
        name="decode_attention",
    )(queries, prefix, suffix, lengths, adapters, down, up)


def solution(mesh):
    return jax.shard_map(
        functools.partial(body, mesh.shape["ctx"], mesh.shape["row"]),
        mesh=mesh,
        in_specs=(
            P("row", None),
            P(None, ("ctx", "row"), None),
            P(None, "row", "ctx", None),
            P("row"),
            P("row", None),
            P("row", "ctx", None),
            P("row", None, "ctx"),
        ),
        out_specs=(P("row", "ctx"), P("row", "ctx")),
        check_vma=False,
    )
```

```python
import functools
import math

import jax
import jax.numpy as jnp
from jax import lax
from jax.experimental import pallas as pl
from jax.experimental.pallas import tpu as pltpu
from jax.sharding import PartitionSpec as P

HD = 128
GROUP = 8
OWN = 4
VEC = 16
EXTRA = 16
COLUMN = 4
NEAR = 4
MESH = pl.DeviceIdType.MESH
F32 = jnp.float32
BF16 = jnp.bfloat16


def three(value):
    high = value.astype(BF16).astype(F32)
    rest = value - high
    middle = rest.astype(BF16).astype(F32)
    return [high, middle, rest - middle]


def stacked(parts, shape, axis):
    at = lax.broadcasted_iota(jnp.int32, shape, axis)
    out = jnp.zeros(shape, F32)
    for index, part in enumerate(parts):
        out = jnp.where(at == index, jnp.broadcast_to(part, shape), out)
    return out


def contract_last(a, b):
    return lax.dot_general(a, b, (((1,), (1,)), ((), ())), preferred_element_type=F32)


def merged(arrived):
    count = arrived.shape[0]
    wide = arrived.astype(F32)
    extra = wide[:, 8:16, :].reshape(count * 8, HD).astype(BF16)
    row = lax.broadcasted_iota(jnp.int32, (HD, 2 * HD), 0)
    col = lax.broadcasted_iota(jnp.int32, (HD, 2 * HD), 1)
    pick = jnp.where(row // 3 == col // HD, 1.0, 0.0).astype(BF16)
    spread = jnp.dot(extra, pick, preferred_element_type=F32)
    tops = spread[:, :HD].reshape(count, 8, HD)
    totals = spread[:, HD:].reshape(count, 8, HD)
    top = jnp.max(tops, axis=0)
    factor = jnp.exp2(tops - top[None])
    return top, jnp.sum(factor * totals, axis=0), jnp.sum(factor * wide[:, 0:8, :], axis=0)


def kernel(
    n_ctx,
    n_row,
    q_hbm,
    kv_hbm,
    suf_hbm,
    len_ref,
    idx_ref,
    down_hbm,
    up_hbm,
    out_ref,
    qv,
    qall,
    qown,
    sufv,
    sx,
    sr,
    kvb,
    vt,
    qb,
    sc,
    ob,
    rb,
    zs,
    zr,
    ad,
    dt,
    ls,
    lr,
    s_q,
    s_suf,
    s_ad_loc,
    s_ad_send,
    s_ad_recv,
    s_a_send,
    s_a_recv,
    s_x_send,
    s_x_recv,
    s_kv_send,
    s_kv_recv,
    s_s_send,
    s_s_recv,
    s_o_send,
    s_o_recv,
    s_z_send,
    s_z_recv,
    s_l_send,
    s_l_recv,
):
    chips = n_ctx // 2
    pairs = chips // 2
    breadth = chips // COLUMN
    lanes = n_row * 8
    pd = kv_hbm.shape[1]
    sd = suf_hbm.shape[1]
    spos = sd // OWN
    scale = HD**-0.5 * math.log2(math.e)

    ctx = lax.axis_index("ctx")
    z = lax.axis_index("row")
    c = lax.rem(ctx, 2)
    groups = n_row // NEAR
    zl = lax.rem(z, NEAR)
    zh = z // NEAR
    chip = ctx // 2
    x = chip // COLUMN
    y = lax.rem(chip, COLUMN)
    sib = ctx + 1 - 2 * c

    owns = y % 2 == x // 2
    lead = jnp.where(owns, x, (x + 2) % COLUMN)
    g0 = 2 * lead + jnp.where(owns, y, (y + 2) % COLUMN) // 2
    seat = 2 * jnp.where(owns, 0, 1) + c

    q_copy = pltpu.make_async_copy(q_hbm, qv, s_q)
    q_copy.start()
    suf_copy = pltpu.make_async_copy(suf_hbm, sufv, s_suf)
    suf_copy.start()
    ad_loc = [
        pltpu.make_async_copy(down_hbm.at[0], ad.at[zl, zh, 0], s_ad_loc.at[0]),
        pltpu.make_async_copy(up_hbm.at[0], ad.at[zl, zh, 1], s_ad_loc.at[1]),
    ]
    for copy in ad_loc:
        copy.start()

    barrier = pltpu.get_barrier_semaphore()

    def greet_line(d, carry):
        pl.semaphore_signal(
            barrier, 1, device_id=(ctx, lax.rem(z + d, n_row)), device_id_type=MESH
        )
        return carry

    def greet_plane(d, carry):
        pl.semaphore_signal(
            barrier, 1, device_id=(lax.rem(ctx + d, n_ctx), z), device_id_type=MESH
        )
        return carry

    lax.fori_loop(1, n_row, greet_line, 0)
    lax.fori_loop(1, n_ctx, greet_plane, 0)

    q_copy.wait()
    queries = qv[...].astype(F32)
    for head in range(pairs * GROUP):
        qall[head * OWN : (head + 1) * OWN, :] = queries[:, head * HD : (head + 1) * HD]
    for side in range(2):
        start = pl.multiple_of(g0 * (GROUP * OWN) + side * VEC + 8 * c, 8)
        qown[side * 8 : (side + 1) * 8, :] = qall[pl.ds(start, 8), :]
    first = pl.ds(pl.multiple_of(z * VEC, VEC), VEC)
    qb[c, first, :] = qown[...].astype(BF16)

    pl.semaphore_wait(barrier, n_ctx - 1 + n_row - 1)

    def send_a(d, carry):
        pltpu.make_async_remote_copy(
            src_ref=qb.at[c, first],
            dst_ref=qb.at[c, first],
            send_sem=s_a_send,
            recv_sem=s_a_recv,
            device_id=(ctx, lax.rem(z + d, n_row)),
            device_id_type=MESH,
        ).start()
        return carry

    lax.fori_loop(1, n_row, send_a, 0)

    def place_kv(i, g):
        home_x = g // 2
        home_y = 2 * (g % 2) + g // 4
        dx = (x - home_x + COLUMN) % COLUMN
        dy = (y - home_y + COLUMN) % COLUMN
        far = jnp.where(dx == 3, 1, dx) + jnp.where(dy == 3, 1, dy)
        level = jnp.where(dx == dy, 1, jnp.where(dx == 2 * (g % 2), 1, 0))
        level = jnp.where(jnp.logical_and(dx % 2 == 1, dx != dy), 0, level)
        stay = jnp.where(far == 2, level, jnp.where(far < 2, 1, 0))
        dx = (dx + 2 * (1 - stay)) % COLUMN
        dy = (dy + 2 * (1 - stay)) % COLUMN
        target_x = (home_x + 2 * (1 - stay)) % COLUMN
        target_y = (home_y + 2 * (1 - stay)) % COLUMN
        one = jnp.where(dy == 0, (dx + 1) // 2, jnp.where(dy == 1, 3, 4))
        two = jnp.where(dx % 2 == 1, 5 + dx // 2, 7)
        near = jnp.logical_or(dx % 2 == 0, dy % 2 == 0)
        near = jnp.logical_and(near, jnp.logical_and(dx != 2, dy != 2))
        slot = jnp.where(near, one, two)
        columns = pl.ds(pl.multiple_of(g * HD, HD), HD)
        return target_x * COLUMN + target_y, slot, kv_hbm.at[i, :, columns]

    for i in range(2):

        def send_kv(d, carry):
            target, slot, part = place_kv(i, lax.rem(g0 + d, pairs))
            pltpu.make_async_remote_copy(
                src_ref=part,
                dst_ref=kvb.at[i, slot],
                send_sem=s_kv_send,
                recv_sem=s_kv_recv.at[i, slot],
                device_id=(target * 2 + c, z),
                device_id_type=MESH,
            ).start()
            return carry

        lax.fori_loop(1, pairs, send_kv, 0)
        _, slot, part = place_kv(i, g0)
        pltpu.make_async_copy(part, kvb.at[i, slot], s_kv_recv.at[i, slot]).start()

    suf_copy.wait()
    at = lax.broadcasted_iota(jnp.int32, (GROUP * OWN, sd), 1)
    row = lax.broadcasted_iota(jnp.int32, (GROUP * OWN, sd), 0)
    owner = at // spos
    live = jnp.zeros((GROUP * OWN, sd), jnp.int32)
    for k in range(OWN):
        live = jnp.where(owner == k, len_ref[k], live)
    valid = (lax.rem(row, OWN) == owner) & (ctx * spos + lax.rem(at, spos) < live)
    for g in range(pairs):
        vectors = qall[g * GROUP * OWN : (g + 1) * GROUP * OWN, :].astype(BF16)
        scores = contract_last(vectors, sufv[0, :, g * HD : (g + 1) * HD]) * scale
        scores = jnp.where(valid, scores, -1e30)
        top = jnp.max(scores, axis=1, keepdims=True)
        weights = jnp.exp2(scores - top)
        total = jnp.sum(weights, axis=1, keepdims=True)
        out = jnp.dot(
            weights.astype(BF16),
            sufv[1, :, g * HD : (g + 1) * HD],
            preferred_element_type=F32,
        )
        extra = stacked(three(top) + three(total), (GROUP * OWN, HD), 1)
        sx[4 * g : 4 * g + 4] = jnp.concatenate(
            [out.reshape(4, 8, HD), extra.reshape(4, 8, HD)], axis=1
        ).astype(BF16)

    def send_s(d, carry):
        target = lax.rem(ctx + d, n_ctx)
        pltpu.make_async_remote_copy(
            src_ref=sx.at[target],
            dst_ref=sr.at[ctx],
            send_sem=s_s_send,
            recv_sem=s_s_recv,
            device_id=(target, z),
            device_id_type=MESH,
        ).start()
        return carry

    lax.fori_loop(1, n_ctx, send_s, 0)
    sr[ctx] = sx[ctx]

    for copy in ad_loc:
        copy.wait()

    def send_far(d, carry):
        pltpu.make_async_remote_copy(
            src_ref=ad.at[zl, zh],
            dst_ref=ad.at[zl, zh],
            send_sem=s_ad_send.at[0],
            recv_sem=s_ad_recv.at[0],
            device_id=(ctx, lax.rem(z + NEAR * d, n_row)),
            device_id_type=MESH,
        ).start()
        return carry

    lax.fori_loop(1, groups, send_far, 0)

    def share_adapters():
        part = ad.at[0, 0 : groups - 1]
        pltpu.make_async_copy(part, part, s_ad_recv.at[0]).wait()
        for d in (1, NEAR - 1, 2):
            pltpu.make_async_remote_copy(
                src_ref=ad.at[zl],
                dst_ref=ad.at[zl],
                send_sem=s_ad_send.at[1],
                recv_sem=s_ad_recv.at[1],
                device_id=(ctx, lax.rem(z + jnp.where(d < NEAR - 1, d, n_row - 1), n_row)),
                device_id_type=MESH,
            ).start()

    def adapters_here():
        part = ad.at[0 : NEAR - 1]
        pltpu.make_async_copy(part, part, s_ad_recv.at[1]).wait()

    def finish(k):
        part = ad.at[0, 0 : groups - 1]
        pltpu.make_async_copy(part, part, s_ad_send.at[0]).wait()
        part = ad.at[0 : NEAR - 1]
        pltpu.make_async_copy(part, part, s_ad_send.at[1]).wait()
        part = qb.at[0, 0 : (n_row - 1) * VEC]
        pltpu.make_async_copy(part, part, s_a_send).wait()
        part = kvb.at[:, 0 : pairs - 1]
        pltpu.make_async_copy(part, part, s_kv_send).wait()
        part = sx.at[0 : n_ctx - 1]
        pltpu.make_async_copy(part, part, s_s_send).wait()
        pltpu.make_async_copy(qb.at[0], qb.at[0], s_x_send).wait()
        part = ob.at[0:3]

        @pl.when(owns)
        def _():
            pltpu.make_async_copy(part, part, s_o_send).wait()

        @pl.when(jnp.logical_not(owns))
        def _():
            pltpu.make_async_copy(ob, ob, s_o_send).wait()

        part = zs.at[0 : n_row - 1]
        pltpu.make_async_copy(part, part, s_z_send).wait()
        part = lr.at[0 : n_ctx - 1]
        pltpu.make_async_copy(part, part, s_l_send).wait()

    part = qb.at[0, 0 : (n_row - 1) * VEC]
    pltpu.make_async_copy(part, part, s_a_recv).wait()
    exchange = pltpu.make_async_remote_copy(
        src_ref=qb.at[c],
        dst_ref=qb.at[c],
        send_sem=s_x_send,
        recv_sem=s_x_recv,
        device_id=(sib, z),
        device_id_type=MESH,
    )
    exchange.start()

    def vectors_of(core):
        wide = qb[core].astype(F32).reshape(n_row, 2, 8, HD)
        return jnp.concatenate(
            [wide[:, side].reshape(lanes, HD) for side in range(2)], axis=0
        ).astype(BF16)

    def arrive(i, j):
        for side in range(2):
            slot = 2 * j + side
            pltpu.make_async_copy(
                kvb.at[i, slot], kvb.at[i, slot], s_kv_recv.at[i, slot]
            ).wait()

    cores = (c, 1 - c)
    tops = []
    for h in range(2):
        if h == 1:
            exchange.wait_recv()
        vectors = vectors_of(cores[h])
        top = None
        for j in range(breadth):
            if h == 0:
                arrive(0, j)
            keys = kvb[0, 2 * j : 2 * j + 2].reshape(2 * pd, HD)
            scores = contract_last(keys, vectors) * scale
            sc[h, j] = scores
            best = jnp.max(scores, axis=0, keepdims=True)
            top = best if top is None else jnp.maximum(top, best)
        tops.append(top)
    for j in range(breadth):
        arrive(1, j)
        vt[j] = kvb[1, 2 * j : 2 * j + 2].reshape(2 * pd, HD).T

    for h in range(2):
        total = jnp.zeros((1, 2 * lanes), F32)
        acc = jnp.zeros((HD, 2 * lanes), F32)
        for j in range(breadth):
            weights = jnp.exp2(sc[h, j] - tops[h])
            total = total + jnp.sum(weights, axis=0, keepdims=True)
            acc = acc + jnp.dot(vt[j], weights.astype(BF16), preferred_element_type=F32)
        extra = stacked(three(tops[h]) + three(total), (EXTRA, 2 * lanes), 0)
        for side in range(2):
            target = (g0 * 2 + side) * 2 + cores[h]
            index = 2 * side + cores[h]
            columns = slice(side * lanes, (side + 1) * lanes)
            ob[index, 0:HD, :] = acc[:, columns].astype(BF16)
            ob[index, HD : HD + EXTRA, :] = extra[:, columns].astype(BF16)

            @pl.when(target != ctx)
            def _():
                pltpu.make_async_remote_copy(
                    src_ref=ob.at[index],
                    dst_ref=rb.at[seat],
                    send_sem=s_o_send,
                    recv_sem=s_o_recv,
                    device_id=(target, z),
                    device_id_type=MESH,
                ).start()

            @pl.when(target == ctx)
            def _():
                pltpu.make_async_copy(ob.at[index], rb.at[seat], s_o_recv).start()

    share_adapters()

    pltpu.make_async_copy(rb, rb, s_o_recv).wait()
    tops, totals = [], []
    for k in range(4):
        extra = rb[k, HD : HD + EXTRA, :].astype(F32)
        tops.append(extra[0:1] + extra[1:2] + extra[2:3])
        totals.append(extra[3:4] + extra[4:5] + extra[5:6])
    top = functools.reduce(jnp.maximum, tops)
    acc = jnp.zeros((HD, lanes), F32)
    total = jnp.zeros((1, lanes), F32)
    for k in range(4):
        factor = jnp.exp2(tops[k] - top)
        acc = acc + factor * rb[k, 0:HD, :].astype(F32)
        total = total + factor * totals[k]
    extra = stacked(three(top) + three(total), (HD, lanes), 0)
    zs[...] = jnp.concatenate(
        [acc.T.reshape(n_row, 8, HD), extra.T.reshape(n_row, 8, HD)], axis=1
    ).astype(BF16)

    def send_z(d, carry):
        target = lax.rem(z + d, n_row)
        pltpu.make_async_remote_copy(
            src_ref=zs.at[target],
            dst_ref=zr.at[z],
            send_sem=s_z_send,
            recv_sem=s_z_recv,
            device_id=(ctx, target),
            device_id_type=MESH,
        ).start()
        return carry

    lax.fori_loop(1, n_row, send_z, 0)
    zr[z] = zs[z]

    part = sr.at[0 : n_ctx - 1]
    pltpu.make_async_copy(part, part, s_s_recv).wait()
    near = merged(sr[...])

    adapters_here()
    rank = down_hbm.shape[1]
    width = n_row * rank // 2
    dt[...] = ad[:, :, 0].reshape(n_row * rank, 2 * HD).T
    row = lax.broadcasted_iota(jnp.int32, (2 * OWN, width), 0)
    col = lax.broadcasted_iota(jnp.int32, (2 * OWN, width), 1)
    wanted = jnp.zeros((2 * OWN, width), jnp.int32)
    for k in range(OWN):
        adapter = idx_ref[0, k]
        wanted = jnp.where(
            lax.rem(row, OWN) == k, (adapter % NEAR) * groups + adapter // NEAR, wanted
        )
    mine = wanted == col // rank + (n_row // 2) * (row // OWN)

    part = zr.at[0 : n_row - 1]
    pltpu.make_async_copy(part, part, s_z_recv).wait()
    far = merged(zr[...])
    top = jnp.maximum(near[0], far[0])
    parts = [jnp.exp2(near[0] - top), jnp.exp2(far[0] - top)]
    total = parts[0] * near[1] + parts[1] * far[1]
    acc = parts[0] * near[2] + parts[1] * far[2]
    attended = (acc / total).astype(BF16).astype(F32)
    attended = jnp.concatenate([attended[0:OWN], attended[OWN : 2 * OWN]], axis=1)
    out_ref[0] = attended.astype(BF16)

    twice = jnp.concatenate([attended, attended], axis=0).astype(BF16)
    low = jnp.dot(twice, dt[...], preferred_element_type=F32)
    low = jnp.where(row < OWN, low[:, :width], low[:, width:])
    ls[...] = jnp.where(mine, low, 0.0)

    def send_l(d, carry):
        pltpu.make_async_remote_copy(
            src_ref=ls,
            dst_ref=lr.at[ctx],
            send_sem=s_l_send,
            recv_sem=s_l_recv,
            device_id=(lax.rem(ctx + d, n_ctx), z),
            device_id_type=MESH,
        ).start()
        return carry

    lax.fori_loop(1, n_ctx, send_l, 0)
    lr[ctx] = ls[...]
    pltpu.make_async_copy(lr.at[0 : n_ctx - 1], lr.at[0 : n_ctx - 1], s_l_recv).wait()
    low = jnp.sum(lr[...], axis=0).astype(BF16)
    up = ad[:, :, 1].reshape(n_row * rank, 2 * HD)
    first = jnp.dot(low, up[:width], preferred_element_type=F32)
    second = jnp.dot(low, up[width:], preferred_element_type=F32)
    delta = first[0:OWN] + second[OWN : 2 * OWN]
    out_ref[1] = (attended + delta.astype(BF16).astype(F32)).astype(BF16)

    finish(99)


def body(n_ctx, n_row, queries, prefix, suffix, lengths, adapters, down, up):
    chips = n_ctx // 2
    pairs = chips // 2
    breadth = chips // COLUMN
    lanes = n_row * 8
    pd = prefix.shape[1]
    sd = suffix.shape[1] * suffix.shape[2]
    width = prefix.shape[2]
    rank = down.shape[2]
    suffix = suffix.reshape(2, sd, width)
    adapters = adapters.T
    down = jnp.transpose(down, (0, 2, 1))
    hbm = pl.BlockSpec(memory_space=pltpu.HBM)
    smem = pl.BlockSpec(memory_space=pltpu.SMEM)
    vmem = pl.BlockSpec(memory_space=pltpu.VMEM)
    dma = pltpu.SemaphoreType.DMA
    both = pl.pallas_call(
        functools.partial(kernel, n_ctx, n_row),
        out_shape=jax.ShapeDtypeStruct((2, OWN, 2 * HD), BF16),
        in_specs=[hbm, hbm, hbm, smem, smem, hbm, hbm],
        out_specs=vmem,
        scratch_shapes=[
            pltpu.VMEM(queries.shape, BF16),
            pltpu.VMEM((pairs * GROUP * OWN, HD), F32),
            pltpu.VMEM((VEC, HD), F32),
            pltpu.VMEM(suffix.shape, BF16),
            pltpu.VMEM((n_ctx, 16, HD), BF16),
            pltpu.VMEM((n_ctx, 16, HD), BF16),
            pltpu.VMEM((2, 2 * breadth, pd, HD), BF16),
            pltpu.VMEM((breadth, HD, 2 * pd), BF16),
            pltpu.VMEM((2, n_row * VEC, HD), BF16),
            pltpu.VMEM((2, breadth, 2 * pd, 2 * lanes), F32),
            pltpu.VMEM((4, HD + EXTRA, lanes), BF16),
            pltpu.VMEM((4, HD + EXTRA, lanes), BF16),
            pltpu.VMEM((n_row, 16, HD), BF16),
            pltpu.VMEM((n_row, 16, HD), BF16),
            pltpu.VMEM((NEAR, n_row // NEAR, 2, rank, 2 * HD), BF16),
            pltpu.VMEM((2 * HD, n_row * rank), BF16),
            pltpu.VMEM((2 * OWN, n_row * rank // 2), F32),
            pltpu.VMEM((n_ctx, 2 * OWN, n_row * rank // 2), F32),
            dma,
            dma,
            dma((2,)),
            dma((2,)),
            dma((2,)),
            dma,
            dma,
            dma,
            dma,
            dma,
            dma((2, 2 * breadth)),
            dma,
            dma,
            dma,
            dma,
            dma,
            dma,
            dma,
            dma,
        ],
        compiler_params=pltpu.CompilerParams(
            collective_id=0, has_side_effects=True, vmem_limit_bytes=64 * 1024 * 1024
        ),
        name="decode_attention",
    )(queries, prefix, suffix, lengths, adapters, down, up)
    return both[0], both[1]


def solution(mesh):
    return jax.shard_map(
        functools.partial(body, mesh.shape["ctx"], mesh.shape["row"]),
        mesh=mesh,
        in_specs=(
            P("row", None),
            P(None, ("ctx", "row"), None),
            P(None, "row", "ctx", None),
            P("row"),
            P("row", None),
            P("row", "ctx", None),
            P("row", None, "ctx"),
        ),
        out_specs=(P("row", "ctx"), P("row", "ctx")),
        check_vma=False,
    )
```

```python
import functools
import math

import jax
import jax.numpy as jnp
from jax import lax
from jax.experimental import pallas as pl
from jax.experimental.pallas import tpu as pltpu
from jax.sharding import PartitionSpec as P

HD = 128
GROUP = 8
OWN = 4
VEC = 16
EXTRA = 16
COLUMN = 4
NEAR = 4
MESH = pl.DeviceIdType.MESH
F32 = jnp.float32
BF16 = jnp.bfloat16


def three(value):
    high = value.astype(BF16).astype(F32)
    rest = value - high
    middle = rest.astype(BF16).astype(F32)
    return [high, middle, rest - middle]


def stacked(parts, shape, axis):
    at = lax.broadcasted_iota(jnp.int32, shape, axis)
    out = jnp.zeros(shape, F32)
    for index, part in enumerate(parts):
        out = jnp.where(at == index, jnp.broadcast_to(part, shape), out)
    return out


def contract_last(a, b):
    return lax.dot_general(a, b, (((1,), (1,)), ((), ())), preferred_element_type=F32)


def merged(arrived):
    count = arrived.shape[0]
    wide = arrived.astype(F32)
    extra = wide[:, 8:16, :].reshape(count * 8, HD).astype(BF16)
    row = lax.broadcasted_iota(jnp.int32, (HD, 2 * HD), 0)
    col = lax.broadcasted_iota(jnp.int32, (HD, 2 * HD), 1)
    pick = jnp.where(row // 3 == col // HD, 1.0, 0.0).astype(BF16)
    spread = jnp.dot(extra, pick, preferred_element_type=F32)
    tops = spread[:, :HD].reshape(count, 8, HD)
    totals = spread[:, HD:].reshape(count, 8, HD)
    top = jnp.max(tops, axis=0)
    factor = jnp.exp2(tops - top[None])
    return top, jnp.sum(factor * totals, axis=0), jnp.sum(factor * wide[:, 0:8, :], axis=0)


def kernel(
    n_ctx,
    n_row,
    q_hbm,
    kv_hbm,
    suf_hbm,
    len_hbm,
    idx_hbm,
    down_hbm,
    up_hbm,
    out_ref,
    len_ref,
    idx_ref,
    qv,
    qall,
    qown,
    sufv,
    sx,
    sr,
    kvb,
    vt,
    qb,
    sc,
    ob,
    rb,
    zs,
    zr,
    ad,
    dt,
    ls,
    lr,
    s_q,
    s_suf,
    s_ad_loc,
    s_ad_send,
    s_ad_recv,
    s_a_send,
    s_a_recv,
    s_kv_send,
    s_kv_recv,
    s_s_send,
    s_s_recv,
    s_o_send,
    s_o_recv,
    s_z_send,
    s_z_recv,
    s_l_send,
    s_l_recv,
):
    chips = n_ctx // 2
    pairs = chips // 2
    breadth = chips // COLUMN
    lanes = n_row * 8
    pd = kv_hbm.shape[1]
    sd = suf_hbm.shape[1]
    spos = sd // OWN
    scale = HD**-0.5 * math.log2(math.e)

    ctx = lax.axis_index("ctx")
    z = lax.axis_index("row")
    c = lax.rem(ctx, 2)
    groups = n_row // NEAR
    zl = lax.rem(z, NEAR)
    zh = z // NEAR
    chip = ctx // 2
    x = chip // COLUMN
    y = lax.rem(chip, COLUMN)
    sib = ctx + 1 - 2 * c

    owns = y % 2 == x // 2
    lead = jnp.where(owns, x, (x + 2) % COLUMN)
    g0 = 2 * lead + jnp.where(owns, y, (y + 2) % COLUMN) // 2
    seat = 2 * jnp.where(owns, 0, 1) + c

    barrier = pltpu.get_barrier_semaphore()

    def greet_line(d, carry):
        target = lax.rem(z + d + jnp.where(d < NEAR, n_row - NEAR, n_row - NEAR + 1), n_row)
        for there in (ctx, sib):
            pl.semaphore_signal(barrier, 1, device_id=(there, target), device_id_type=MESH)
        return carry

    def greet_plane(d, carry):
        pl.semaphore_signal(
            barrier, 1, device_id=(lax.rem(ctx + d, n_ctx), z), device_id_type=MESH
        )
        return carry

    lax.fori_loop(0, 2 * NEAR, greet_line, 0)
    lax.fori_loop(1, n_ctx, greet_plane, 0)

    q_copy = pltpu.make_async_copy(q_hbm, qv, s_q)
    q_copy.start()
    suf_copy = pltpu.make_async_copy(suf_hbm, sufv, s_suf)
    suf_copy.start()
    ad_loc = [
        pltpu.make_async_copy(down_hbm.at[0], ad.at[zl, zh, 0], s_ad_loc.at[0]),
        pltpu.make_async_copy(up_hbm.at[0], ad.at[zl, zh, 1], s_ad_loc.at[1]),
    ]
    ad_loc.append(pltpu.make_async_copy(len_hbm, len_ref, s_ad_loc.at[2]))
    ad_loc.append(pltpu.make_async_copy(idx_hbm, idx_ref, s_ad_loc.at[3]))
    for copy in ad_loc:
        copy.start()

    q_copy.wait()
    queries = qv[...].astype(F32)
    for head in range(pairs * GROUP):
        qall[head * OWN : (head + 1) * OWN, :] = queries[:, head * HD : (head + 1) * HD]
    for side in range(2):
        start = pl.multiple_of(g0 * (GROUP * OWN) + side * VEC + 8 * c, 8)
        qown[side * 8 : (side + 1) * 8, :] = qall[pl.ds(start, 8), :]
    qb[c, 0:VEC, :] = qown[...].astype(BF16)

    pl.semaphore_wait(barrier, n_ctx - 1 + 4 * NEAR)

    def send_q(first, count, place, there, step, sems):
        pltpu.make_async_remote_copy(
            src_ref=qb.at[c, first * VEC : (first + count) * VEC],
            dst_ref=qb.at[c, place * VEC : (place + count) * VEC],
            send_sem=s_a_send.at[sems // 2],
            recv_sem=s_a_recv.at[c, sems],
            device_id=(there, lax.rem(z + step + n_row, n_row)),
            device_id_type=MESH,
        ).start()

    def wait_q(core, kind, count):
        part = qb.at[0, 0 : count * VEC]
        pltpu.make_async_copy(part, part, s_a_recv.at[core, kind]).wait()

    for d in range(NEAR, 0, -1):
        for there in (ctx, sib):
            send_q(0, 1, n_row - d, there, d, 0)
        if d < NEAR:
            for there in (ctx, sib):
                send_q(0, 1, d, there, -d, 1)
    send_q(0, 1, 0, sib, 0, 1)

    def place_kv(i, g):
        home_x = g // 2
        home_y = 2 * (g % 2) + g // 4
        dx = (x - home_x + COLUMN) % COLUMN
        dy = (y - home_y + COLUMN) % COLUMN
        far = jnp.where(dx == 3, 1, dx) + jnp.where(dy == 3, 1, dy)
        level = jnp.where(dx == dy, 1, jnp.where(dx == 2 * (g % 2), 1, 0))
        level = jnp.where(jnp.logical_and(dx % 2 == 1, dx != dy), 0, level)
        stay = jnp.where(far == 2, level, jnp.where(far < 2, 1, 0))
        dx = (dx + 2 * (1 - stay)) % COLUMN
        dy = (dy + 2 * (1 - stay)) % COLUMN
        target_x = (home_x + 2 * (1 - stay)) % COLUMN
        target_y = (home_y + 2 * (1 - stay)) % COLUMN
        one = jnp.where(dy == 0, (dx + 1) // 2, jnp.where(dy == 1, 3, 4))
        two = jnp.where(dx % 2 == 1, 5 + dx // 2, 7)
        near = jnp.logical_or(dx % 2 == 0, dy % 2 == 0)
        near = jnp.logical_and(near, jnp.logical_and(dx != 2, dy != 2))
        slot = jnp.where(near, one, two)
        columns = pl.ds(pl.multiple_of(g * HD, HD), HD)
        return target_x * COLUMN + target_y, slot, kv_hbm.at[i, :, columns]

    for i in range(2):

        def send_kv(d, carry):
            target, slot, part = place_kv(i, lax.rem(g0 + d, pairs))
            pltpu.make_async_remote_copy(
                src_ref=part,
                dst_ref=kvb.at[i, slot],
                send_sem=s_kv_send,
                recv_sem=s_kv_recv.at[i, slot],
                device_id=(target * 2 + c, z),
                device_id_type=MESH,
            ).start()
            return carry

        lax.fori_loop(1, pairs, send_kv, 0)
        _, slot, part = place_kv(i, g0)
        pltpu.make_async_copy(part, kvb.at[i, slot], s_kv_recv.at[i, slot]).start()

    wait_q(c, 0, NEAR)
    for there in (ctx, sib):
        send_q(n_row - NEAR, NEAR, n_row - 2 * NEAR, there, NEAR, 2)
    wait_q(c, 1, NEAR - 1)
    for there in (ctx, sib):
        send_q(0, NEAR, NEAR, there, -NEAR, 2)

    suf_copy.wait()
    for copy in ad_loc:
        copy.wait()
    at = lax.broadcasted_iota(jnp.int32, (GROUP * OWN, sd), 1)
    row = lax.broadcasted_iota(jnp.int32, (GROUP * OWN, sd), 0)
    owner = at // spos
    live = jnp.zeros((GROUP * OWN, sd), jnp.int32)
    for k in range(OWN):
        live = jnp.where(owner == k, len_ref[k], live)
    valid = (lax.rem(row, OWN) == owner) & (ctx * spos + lax.rem(at, spos) < live)
    for g in range(pairs):
        vectors = qall[g * GROUP * OWN : (g + 1) * GROUP * OWN, :].astype(BF16)
        scores = contract_last(vectors, sufv[0, :, g * HD : (g + 1) * HD]) * scale
        scores = jnp.where(valid, scores, -1e30)
        top = jnp.max(scores, axis=1, keepdims=True)
        weights = jnp.exp2(scores - top)
        total = jnp.sum(weights, axis=1, keepdims=True)
        out = jnp.dot(
            weights.astype(BF16),
            sufv[1, :, g * HD : (g + 1) * HD],
            preferred_element_type=F32,
        )
        extra = stacked(three(top) + three(total), (GROUP * OWN, HD), 1)
        sx[4 * g : 4 * g + 4] = jnp.concatenate(
            [out.reshape(4, 8, HD), extra.reshape(4, 8, HD)], axis=1
        ).astype(BF16)

    def send_s(d, carry):
        target = lax.rem(ctx + d, n_ctx)
        pltpu.make_async_remote_copy(
            src_ref=sx.at[target],
            dst_ref=sr.at[ctx],
            send_sem=s_s_send,
            recv_sem=s_s_recv,
            device_id=(target, z),
            device_id_type=MESH,
        ).start()
        return carry

    lax.fori_loop(1, n_ctx, send_s, 0)
    sr[ctx] = sx[ctx]

    def send_far(d, carry):
        pltpu.make_async_remote_copy(
            src_ref=ad.at[zl, zh],
            dst_ref=ad.at[zl, zh],
            send_sem=s_ad_send.at[0],
            recv_sem=s_ad_recv.at[0],
            device_id=(ctx, lax.rem(z + NEAR * d, n_row)),
            device_id_type=MESH,
        ).start()
        return carry


    def share_adapters():
        part = ad.at[0, 0 : groups - 1]
        pltpu.make_async_copy(part, part, s_ad_recv.at[0]).wait()
        for d in (1, NEAR - 1, 2):
            pltpu.make_async_remote_copy(
                src_ref=ad.at[zl],
                dst_ref=ad.at[zl],
                send_sem=s_ad_send.at[1],
                recv_sem=s_ad_recv.at[1],
                device_id=(ctx, lax.rem(z + jnp.where(d < NEAR - 1, d, n_row - 1), n_row)),
                device_id_type=MESH,
            ).start()

    def adapters_here():
        part = ad.at[0 : NEAR - 1]
        pltpu.make_async_copy(part, part, s_ad_recv.at[1]).wait()

    def finish(k):
        part = ad.at[0, 0 : groups - 1]
        pltpu.make_async_copy(part, part, s_ad_send.at[0]).wait()
        part = ad.at[0 : NEAR - 1]
        pltpu.make_async_copy(part, part, s_ad_send.at[1]).wait()
        part = qb.at[0, 0 : (4 * NEAR - 1) * VEC]
        pltpu.make_async_copy(part, part, s_a_send.at[0]).wait()
        part = qb.at[0, 0 : 4 * NEAR * VEC]
        pltpu.make_async_copy(part, part, s_a_send.at[1]).wait()
        part = kvb.at[:, 0 : pairs - 1]
        pltpu.make_async_copy(part, part, s_kv_send).wait()
        part = sx.at[0 : n_ctx - 1]
        pltpu.make_async_copy(part, part, s_s_send).wait()
        part = ob.at[0:3]

        @pl.when(owns)
        def _():
            pltpu.make_async_copy(part, part, s_o_send).wait()

        @pl.when(jnp.logical_not(owns))
        def _():
            pltpu.make_async_copy(ob, ob, s_o_send).wait()

        part = zs.at[0 : n_row - 1]
        pltpu.make_async_copy(part, part, s_z_send).wait()
        part = lr.at[0 : n_ctx - 1]
        pltpu.make_async_copy(part, part, s_l_send).wait()

    wait_q(c, 2, 2 * NEAR)
    lax.fori_loop(1, groups, send_far, 0)

    def vectors_of(core):
        wide = qb[core].astype(F32).reshape(n_row, 2, 8, HD)
        return jnp.concatenate(
            [wide[:, side].reshape(lanes, HD) for side in range(2)], axis=0
        ).astype(BF16)

    def arrive(i, j):
        for side in range(2):
            slot = 2 * j + side
            pltpu.make_async_copy(
                kvb.at[i, slot], kvb.at[i, slot], s_kv_recv.at[i, slot]
            ).wait()

    cores = (c, 1 - c)
    tops = []
    for h in range(2):
        if h == 1:
            wait_q(1 - c, 0, NEAR)
            wait_q(1 - c, 1, NEAR)
            wait_q(1 - c, 2, 2 * NEAR)
        vectors = vectors_of(cores[h])
        top = None
        for j in range(breadth):
            if h == 0:
                arrive(0, j)
            keys = kvb[0, 2 * j : 2 * j + 2].reshape(2 * pd, HD)
            scores = contract_last(keys, vectors) * scale
            sc[h, j] = scores
            best = jnp.max(scores, axis=0, keepdims=True)
            top = best if top is None else jnp.maximum(top, best)
        tops.append(top)
    for j in range(breadth):
        arrive(1, j)
        vt[j] = kvb[1, 2 * j : 2 * j + 2].reshape(2 * pd, HD).T

    for h in range(2):
        total = jnp.zeros((1, 2 * lanes), F32)
        acc = jnp.zeros((HD, 2 * lanes), F32)
        for j in range(breadth):
            weights = jnp.exp2(sc[h, j] - tops[h])
            total = total + jnp.sum(weights, axis=0, keepdims=True)
            acc = acc + jnp.dot(vt[j], weights.astype(BF16), preferred_element_type=F32)
        extra = stacked(three(tops[h]) + three(total), (EXTRA, 2 * lanes), 0)
        for side in range(2):
            target = (g0 * 2 + side) * 2 + cores[h]
            index = 2 * side + cores[h]
            columns = slice(side * lanes, (side + 1) * lanes)
            ob[index, 0:HD, :] = acc[:, columns].astype(BF16)
            ob[index, HD : HD + EXTRA, :] = extra[:, columns].astype(BF16)

            @pl.when(target != ctx)
            def _():
                pltpu.make_async_remote_copy(
                    src_ref=ob.at[index],
                    dst_ref=rb.at[seat],
                    send_sem=s_o_send,
                    recv_sem=s_o_recv,
                    device_id=(target, z),
                    device_id_type=MESH,
                ).start()

            @pl.when(target == ctx)
            def _():
                pltpu.make_async_copy(ob.at[index], rb.at[seat], s_o_recv).start()

    pltpu.make_async_copy(rb, rb, s_o_recv).wait()
    tops, totals = [], []
    for k in range(4):
        extra = rb[k, HD : HD + EXTRA, :].astype(F32)
        tops.append(extra[0:1] + extra[1:2] + extra[2:3])
        totals.append(extra[3:4] + extra[4:5] + extra[5:6])
    top = functools.reduce(jnp.maximum, tops)
    acc = jnp.zeros((HD, lanes), F32)
    total = jnp.zeros((1, lanes), F32)
    for k in range(4):
        factor = jnp.exp2(tops[k] - top)
        acc = acc + factor * rb[k, 0:HD, :].astype(F32)
        total = total + factor * totals[k]
    extra = stacked(three(top) + three(total), (HD, lanes), 0)
    zs[...] = jnp.concatenate(
        [acc.T.reshape(n_row, 8, HD), extra.T.reshape(n_row, 8, HD)], axis=1
    ).astype(BF16)

    def send_z(i, carry):
        step = n_row // 2 + jnp.where(i % 2 == 0, -(i // 2), i // 2)
        pltpu.make_async_remote_copy(
            src_ref=zs.at[step],
            dst_ref=zr.at[z],
            send_sem=s_z_send,
            recv_sem=s_z_recv,
            device_id=(ctx, lax.rem(z + step, n_row)),
            device_id_type=MESH,
        ).start()
        return carry

    lax.fori_loop(1, n_row, send_z, 0)
    zr[z] = zs[0]
    share_adapters()

    part = sr.at[0 : n_ctx - 1]
    pltpu.make_async_copy(part, part, s_s_recv).wait()
    near = merged(sr[...])

    adapters_here()
    rank = down_hbm.shape[1]
    width = n_row * rank // 2
    dt[...] = ad[:, :, 0].reshape(n_row * rank, 2 * HD).T
    row = lax.broadcasted_iota(jnp.int32, (2 * OWN, width), 0)
    col = lax.broadcasted_iota(jnp.int32, (2 * OWN, width), 1)
    wanted = jnp.zeros((2 * OWN, width), jnp.int32)
    for k in range(OWN):
        adapter = idx_ref[0, k]
        wanted = jnp.where(
            lax.rem(row, OWN) == k, (adapter % NEAR) * groups + adapter // NEAR, wanted
        )
    mine = wanted == col // rank + (n_row // 2) * (row // OWN)

    part = zr.at[0 : n_row - 1]
    pltpu.make_async_copy(part, part, s_z_recv).wait()
    far = merged(zr[...])
    top = jnp.maximum(near[0], far[0])
    parts = [jnp.exp2(near[0] - top), jnp.exp2(far[0] - top)]
    total = parts[0] * near[1] + parts[1] * far[1]
    acc = parts[0] * near[2] + parts[1] * far[2]
    attended = (acc / total).astype(BF16).astype(F32)
    attended = jnp.concatenate([attended[0:OWN], attended[OWN : 2 * OWN]], axis=1)
    out_ref[0] = attended.astype(BF16)

    twice = jnp.concatenate([attended, attended], axis=0).astype(BF16)
    low = jnp.dot(twice, dt[...], preferred_element_type=F32)
    low = jnp.where(row < OWN, low[:, :width], low[:, width:])
    ls[...] = jnp.where(mine, low, 0.0)

    def send_l(d, carry):
        pltpu.make_async_remote_copy(
            src_ref=ls,
            dst_ref=lr.at[ctx],
            send_sem=s_l_send,
            recv_sem=s_l_recv,
            device_id=(lax.rem(ctx + d, n_ctx), z),
            device_id_type=MESH,
        ).start()
        return carry

    lax.fori_loop(1, n_ctx, send_l, 0)
    lr[ctx] = ls[...]
    pltpu.make_async_copy(lr.at[0 : n_ctx - 1], lr.at[0 : n_ctx - 1], s_l_recv).wait()
    low = jnp.sum(lr[...], axis=0).astype(BF16)
    up = ad[:, :, 1].reshape(n_row * rank, 2 * HD)
    first = jnp.dot(low, up[:width], preferred_element_type=F32)
    second = jnp.dot(low, up[width:], preferred_element_type=F32)
    delta = first[0:OWN] + second[OWN : 2 * OWN]
    out_ref[1] = (attended + delta.astype(BF16).astype(F32)).astype(BF16)

    finish(99)


def body(n_ctx, n_row, queries, prefix, suffix, lengths, adapters, down, up):
    chips = n_ctx // 2
    pairs = chips // 2
    breadth = chips // COLUMN
    lanes = n_row * 8
    pd = prefix.shape[1]
    sd = suffix.shape[1] * suffix.shape[2]
    width = prefix.shape[2]
    rank = down.shape[2]
    suffix = suffix.reshape(2, sd, width)
    adapters = adapters.T
    down = jnp.transpose(down, (0, 2, 1))
    hbm = pl.BlockSpec(memory_space=pltpu.HBM)
    vmem = pl.BlockSpec(memory_space=pltpu.VMEM)
    dma = pltpu.SemaphoreType.DMA
    both = pl.pallas_call(
        functools.partial(kernel, n_ctx, n_row),
        out_shape=jax.ShapeDtypeStruct((2, OWN, 2 * HD), BF16),
        in_specs=[hbm] * 7,
        out_specs=vmem,
        scratch_shapes=[
            pltpu.SMEM(lengths.shape, jnp.int32),
            pltpu.SMEM(adapters.shape, jnp.int32),
            pltpu.VMEM(queries.shape, BF16),
            pltpu.VMEM((pairs * GROUP * OWN, HD), F32),
            pltpu.VMEM((VEC, HD), F32),
            pltpu.VMEM(suffix.shape, BF16),
            pltpu.VMEM((n_ctx, 16, HD), BF16),
            pltpu.VMEM((n_ctx, 16, HD), BF16),
            pltpu.VMEM((2, 2 * breadth, pd, HD), BF16),
            pltpu.VMEM((breadth, HD, 2 * pd), BF16),
            pltpu.VMEM((2, n_row * VEC, HD), BF16),
            pltpu.VMEM((2, breadth, 2 * pd, 2 * lanes), F32),
            pltpu.VMEM((4, HD + EXTRA, lanes), BF16),
            pltpu.VMEM((4, HD + EXTRA, lanes), BF16),
            pltpu.VMEM((n_row, 16, HD), BF16),
            pltpu.VMEM((n_row, 16, HD), BF16),
            pltpu.VMEM((NEAR, n_row // NEAR, 2, rank, 2 * HD), BF16),
            pltpu.VMEM((2 * HD, n_row * rank), BF16),
            pltpu.VMEM((2 * OWN, n_row * rank // 2), F32),
            pltpu.VMEM((n_ctx, 2 * OWN, n_row * rank // 2), F32),
            dma,
            dma,
            dma((4,)),
            dma((2,)),
            dma((2,)),
            dma((2,)),
            dma((2, 3)),
            dma,
            dma((2, 2 * breadth)),
            dma,
            dma,
            dma,
            dma,
            dma,
            dma,
            dma,
            dma,
        ],
        compiler_params=pltpu.CompilerParams(
            collective_id=0, has_side_effects=True, vmem_limit_bytes=64 * 1024 * 1024
        ),
        name="decode_attention",
    )(queries, prefix, suffix, lengths, adapters, down, up)
    return both[0], both[1]


def solution(mesh):
    return jax.shard_map(
        functools.partial(body, mesh.shape["ctx"], mesh.shape["row"]),
        mesh=mesh,
        in_specs=(
            P("row", None),
            P(None, ("ctx", "row"), None),
            P(None, "row", "ctx", None),
            P("row"),
            P("row", None),
            P("row", "ctx", None),
            P("row", None, "ctx"),
        ),
        out_specs=(P("row", "ctx"), P("row", "ctx")),
        check_vma=False,
    )
```

```python
import functools
import math

import jax
import jax.numpy as jnp
from jax import lax
from jax.experimental import pallas as pl
from jax.experimental.pallas import tpu as pltpu
from jax.sharding import PartitionSpec as P

HD = 128
GROUP = 8
OWN = 4
VEC = 16
EXTRA = 16
COLUMN = 4
NEAR = 4
MESH = pl.DeviceIdType.MESH
F32 = jnp.float32
BF16 = jnp.bfloat16


def three(value):
    high = value.astype(BF16).astype(F32)
    rest = value - high
    middle = rest.astype(BF16).astype(F32)
    return [high, middle, rest - middle]


def stacked(parts, shape, axis):
    at = lax.broadcasted_iota(jnp.int32, shape, axis)
    out = jnp.zeros(shape, F32)
    for index, part in enumerate(parts):
        out = jnp.where(at == index, jnp.broadcast_to(part, shape), out)
    return out


def contract_last(a, b):
    return lax.dot_general(a, b, (((1,), (1,)), ((), ())), preferred_element_type=F32)


def merged(arrived):
    count = arrived.shape[0]
    wide = arrived.astype(F32)
    extra = wide[:, 8:16, :].reshape(count * 8, HD).astype(BF16)
    row = lax.broadcasted_iota(jnp.int32, (HD, 2 * HD), 0)
    col = lax.broadcasted_iota(jnp.int32, (HD, 2 * HD), 1)
    pick = jnp.where(row // 3 == col // HD, 1.0, 0.0).astype(BF16)
    spread = jnp.dot(extra, pick, preferred_element_type=F32)
    tops = spread[:, :HD].reshape(count, 8, HD)
    totals = spread[:, HD:].reshape(count, 8, HD)
    top = jnp.max(tops, axis=0)
    factor = jnp.exp2(tops - top[None])
    return top, jnp.sum(factor * totals, axis=0), jnp.sum(factor * wide[:, 0:8, :], axis=0)


def kernel(
    n_ctx,
    n_row,
    q_hbm,
    kv_hbm,
    suf_hbm,
    len_hbm,
    idx_hbm,
    down_hbm,
    up_hbm,
    out_ref,
    len_ref,
    idx_ref,
    qv,
    qall,
    qown,
    sufv,
    sx,
    sr,
    kvb,
    vt,
    qb,
    sc,
    ob,
    rb,
    zs,
    zr,
    ad,
    dt,
    ls,
    lr,
    s_q,
    s_suf,
    s_ad_loc,
    s_ad_send,
    s_ad_recv,
    s_a_send,
    s_a_recv,
    s_kv_send,
    s_kv_recv,
    s_s_send,
    s_s_recv,
    s_o_send,
    s_o_recv,
    s_z_send,
    s_z_recv,
    s_l_send,
    s_l_recv,
):
    chips = n_ctx // 2
    pairs = chips // 2
    breadth = chips // COLUMN
    lanes = n_row * 8
    pd = kv_hbm.shape[1]
    sd = suf_hbm.shape[1]
    spos = sd // OWN
    scale = HD**-0.5 * math.log2(math.e)

    ctx = lax.axis_index("ctx")
    z = lax.axis_index("row")
    c = lax.rem(ctx, 2)
    groups = n_row // NEAR
    zl = lax.rem(z, NEAR)
    zh = z // NEAR
    chip = ctx // 2
    x = chip // COLUMN
    y = lax.rem(chip, COLUMN)
    sib = ctx + 1 - 2 * c

    owns = y % 2 == x // 2
    lead = jnp.where(owns, x, (x + 2) % COLUMN)
    g0 = 2 * lead + jnp.where(owns, y, (y + 2) % COLUMN) // 2
    seat = 2 * jnp.where(owns, 0, 1) + c

    barrier = pltpu.get_barrier_semaphore()

    def greet_line(d, carry):
        target = lax.rem(z + d + jnp.where(d < NEAR, n_row - NEAR, n_row - NEAR + 1), n_row)
        for there in (ctx, sib):
            pl.semaphore_signal(barrier, 1, device_id=(there, target), device_id_type=MESH)
        return carry

    def greet_plane(d, carry):
        pl.semaphore_signal(
            barrier, 1, device_id=(lax.rem(ctx + d, n_ctx), z), device_id_type=MESH
        )
        return carry

    lax.fori_loop(0, 2 * NEAR, greet_line, 0)
    lax.fori_loop(1, n_ctx, greet_plane, 0)

    q_copy = pltpu.make_async_copy(q_hbm, qv, s_q)
    q_copy.start()
    suf_copy = pltpu.make_async_copy(suf_hbm, sufv, s_suf)
    suf_copy.start()
    ad_loc = [
        pltpu.make_async_copy(down_hbm.at[0], ad.at[zl, zh, 0], s_ad_loc.at[0]),
        pltpu.make_async_copy(up_hbm.at[0], ad.at[zl, zh, 1], s_ad_loc.at[1]),
    ]
    ad_loc.append(pltpu.make_async_copy(len_hbm, len_ref, s_ad_loc.at[2]))
    ad_loc.append(pltpu.make_async_copy(idx_hbm, idx_ref, s_ad_loc.at[3]))
    for copy in ad_loc:
        copy.start()

    q_copy.wait()
    queries = qv[...].astype(F32)
    for head in range(pairs * GROUP):
        qall[head * OWN : (head + 1) * OWN, :] = queries[:, head * HD : (head + 1) * HD]
    for side in range(2):
        start = pl.multiple_of(g0 * (GROUP * OWN) + side * VEC + 8 * c, 8)
        qown[side * 8 : (side + 1) * 8, :] = qall[pl.ds(start, 8), :]
    qb[c, 0:VEC, :] = qown[...].astype(BF16)

    pl.semaphore_wait(barrier, n_ctx - 1 + 4 * NEAR)

    def send_q(first, count, place, there, step, sems):
        pltpu.make_async_remote_copy(
            src_ref=qb.at[c, first * VEC : (first + count) * VEC],
            dst_ref=qb.at[c, place * VEC : (place + count) * VEC],
            send_sem=s_a_send.at[sems // 2],
            recv_sem=s_a_recv.at[c, sems],
            device_id=(there, lax.rem(z + step + n_row, n_row)),
            device_id_type=MESH,
        ).start()

    def wait_q(core, kind, count):
        part = qb.at[0, 0 : count * VEC]
        pltpu.make_async_copy(part, part, s_a_recv.at[core, kind]).wait()

    for d in range(NEAR, 0, -1):
        for there in (ctx, sib):
            send_q(0, 1, n_row - d, there, d, 0)
        if d < NEAR:
            for there in (ctx, sib):
                send_q(0, 1, d, there, -d, 1)
    send_q(0, 1, 0, sib, 0, 1)

    def send_far(block, step, kind):
        pltpu.make_async_remote_copy(
            src_ref=ad.at[zl, block],
            dst_ref=ad.at[zl, block],
            send_sem=s_ad_send.at[kind],
            recv_sem=s_ad_recv.at[kind],
            device_id=(ctx, lax.rem(z + step + n_row, n_row)),
            device_id_type=MESH,
        ).start()

    def pass_adapters():
        part = ad.at[0, 0:2]
        pltpu.make_async_copy(part, part, s_ad_recv.at[0]).wait()
        send_far(lax.rem(zh + groups - 1, groups), NEAR, 1)

    def share_adapters():
        part = ad.at[0, 0]
        pltpu.make_async_copy(part, part, s_ad_recv.at[1]).wait()
        for d in (1, n_row - 1, 2):
            pltpu.make_async_remote_copy(
                src_ref=ad.at[zl],
                dst_ref=ad.at[zl],
                send_sem=s_ad_send.at[2],
                recv_sem=s_ad_recv.at[2],
                device_id=(ctx, lax.rem(z + d, n_row)),
                device_id_type=MESH,
            ).start()

    for copy in ad_loc:
        copy.wait()
    send_far(zh, NEAR, 0)
    send_far(zh, -NEAR, 0)

    def place_kv(i, g):
        home_x = g // 2
        home_y = 2 * (g % 2) + g // 4
        dx = (x - home_x + COLUMN) % COLUMN
        dy = (y - home_y + COLUMN) % COLUMN
        far = jnp.where(dx == 3, 1, dx) + jnp.where(dy == 3, 1, dy)
        level = jnp.where(dx == dy, 1, jnp.where(dx == 2 * (g % 2), 1, 0))
        level = jnp.where(jnp.logical_and(dx % 2 == 1, dx != dy), 0, level)
        stay = jnp.where(far == 2, level, jnp.where(far < 2, 1, 0))
        dx = (dx + 2 * (1 - stay)) % COLUMN
        dy = (dy + 2 * (1 - stay)) % COLUMN
        target_x = (home_x + 2 * (1 - stay)) % COLUMN
        target_y = (home_y + 2 * (1 - stay)) % COLUMN
        one = jnp.where(dy == 0, (dx + 1) // 2, jnp.where(dy == 1, 3, 4))
        two = jnp.where(dx % 2 == 1, 5 + dx // 2, 7)
        near = jnp.logical_or(dx % 2 == 0, dy % 2 == 0)
        near = jnp.logical_and(near, jnp.logical_and(dx != 2, dy != 2))
        slot = jnp.where(near, one, two)
        columns = pl.ds(pl.multiple_of(g * HD, HD), HD)
        return target_x * COLUMN + target_y, slot, kv_hbm.at[i, :, columns]

    for i in range(2):

        def send_kv(d, carry):
            target, slot, part = place_kv(i, lax.rem(g0 + d, pairs))
            pltpu.make_async_remote_copy(
                src_ref=part,
                dst_ref=kvb.at[i, slot],
                send_sem=s_kv_send,
                recv_sem=s_kv_recv.at[i, slot],
                device_id=(target * 2 + c, z),
                device_id_type=MESH,
            ).start()
            return carry

        lax.fori_loop(1, pairs, send_kv, 0)
        _, slot, part = place_kv(i, g0)
        pltpu.make_async_copy(part, kvb.at[i, slot], s_kv_recv.at[i, slot]).start()

    wait_q(c, 0, NEAR)
    for there in (ctx, sib):
        send_q(n_row - NEAR, NEAR, n_row - 2 * NEAR, there, NEAR, 2)
    wait_q(c, 1, NEAR - 1)
    for there in (ctx, sib):
        send_q(0, NEAR, NEAR, there, -NEAR, 2)

    suf_copy.wait()
    at = lax.broadcasted_iota(jnp.int32, (GROUP * OWN, sd), 1)
    row = lax.broadcasted_iota(jnp.int32, (GROUP * OWN, sd), 0)
    owner = at // spos
    live = jnp.zeros((GROUP * OWN, sd), jnp.int32)
    for k in range(OWN):
        live = jnp.where(owner == k, len_ref[k], live)
    valid = (lax.rem(row, OWN) == owner) & (ctx * spos + lax.rem(at, spos) < live)
    for g in range(pairs):
        vectors = qall[g * GROUP * OWN : (g + 1) * GROUP * OWN, :].astype(BF16)
        scores = contract_last(vectors, sufv[0, :, g * HD : (g + 1) * HD]) * scale
        scores = jnp.where(valid, scores, -1e30)
        top = jnp.max(scores, axis=1, keepdims=True)
        weights = jnp.exp2(scores - top)
        total = jnp.sum(weights, axis=1, keepdims=True)
        out = jnp.dot(
            weights.astype(BF16),
            sufv[1, :, g * HD : (g + 1) * HD],
            preferred_element_type=F32,
        )
        extra = stacked(three(top) + three(total), (GROUP * OWN, HD), 1)
        sx[4 * g : 4 * g + 4] = jnp.concatenate(
            [out.reshape(4, 8, HD), extra.reshape(4, 8, HD)], axis=1
        ).astype(BF16)

    def send_s(d, carry):
        target = lax.rem(ctx + d, n_ctx)
        pltpu.make_async_remote_copy(
            src_ref=sx.at[target],
            dst_ref=sr.at[ctx],
            send_sem=s_s_send,
            recv_sem=s_s_recv,
            device_id=(target, z),
            device_id_type=MESH,
        ).start()
        return carry

    lax.fori_loop(1, n_ctx, send_s, 0)
    sr[ctx] = sx[ctx]

    def adapters_here():
        part = ad.at[0 : NEAR - 1]
        pltpu.make_async_copy(part, part, s_ad_recv.at[2]).wait()

    def finish(k):
        part = ad.at[0, 0:2]
        pltpu.make_async_copy(part, part, s_ad_send.at[0]).wait()
        part = ad.at[0, 0]
        pltpu.make_async_copy(part, part, s_ad_send.at[1]).wait()
        part = ad.at[0 : NEAR - 1]
        pltpu.make_async_copy(part, part, s_ad_send.at[2]).wait()
        part = qb.at[0, 0 : (4 * NEAR - 1) * VEC]
        pltpu.make_async_copy(part, part, s_a_send.at[0]).wait()
        part = qb.at[0, 0 : 4 * NEAR * VEC]
        pltpu.make_async_copy(part, part, s_a_send.at[1]).wait()
        part = kvb.at[:, 0 : pairs - 1]
        pltpu.make_async_copy(part, part, s_kv_send).wait()
        part = sx.at[0 : n_ctx - 1]
        pltpu.make_async_copy(part, part, s_s_send).wait()
        part = ob.at[0:3]

        @pl.when(owns)
        def _():
            pltpu.make_async_copy(part, part, s_o_send).wait()

        @pl.when(jnp.logical_not(owns))
        def _():
            pltpu.make_async_copy(ob, ob, s_o_send).wait()

        part = zs.at[0 : n_row - 1]
        pltpu.make_async_copy(part, part, s_z_send).wait()
        part = lr.at[0 : n_ctx - 1]
        pltpu.make_async_copy(part, part, s_l_send).wait()

    wait_q(c, 2, 2 * NEAR)
    pass_adapters()

    def vectors_of(core):
        wide = qb[core].astype(F32).reshape(n_row, 2, 8, HD)
        return jnp.concatenate(
            [wide[:, side].reshape(lanes, HD) for side in range(2)], axis=0
        ).astype(BF16)

    def arrive(i, j):
        for side in range(2):
            slot = 2 * j + side
            pltpu.make_async_copy(
                kvb.at[i, slot], kvb.at[i, slot], s_kv_recv.at[i, slot]
            ).wait()

    cores = (c, 1 - c)
    tops = []
    for h in range(2):
        if h == 1:
            wait_q(1 - c, 0, NEAR)
            wait_q(1 - c, 1, NEAR)
            wait_q(1 - c, 2, 2 * NEAR)
        vectors = vectors_of(cores[h])
        top = None
        for j in range(breadth):
            if h == 0:
                arrive(0, j)
            keys = kvb[0, 2 * j : 2 * j + 2].reshape(2 * pd, HD)
            scores = contract_last(keys, vectors) * scale
            sc[h, j] = scores
            best = jnp.max(scores, axis=0, keepdims=True)
            top = best if top is None else jnp.maximum(top, best)
        tops.append(top)
    for j in range(breadth):
        arrive(1, j)
        vt[j] = kvb[1, 2 * j : 2 * j + 2].reshape(2 * pd, HD).T

    for h in range(2):
        total = jnp.zeros((1, 2 * lanes), F32)
        acc = jnp.zeros((HD, 2 * lanes), F32)
        for j in range(breadth):
            weights = jnp.exp2(sc[h, j] - tops[h])
            total = total + jnp.sum(weights, axis=0, keepdims=True)
            acc = acc + jnp.dot(vt[j], weights.astype(BF16), preferred_element_type=F32)
        extra = stacked(three(tops[h]) + three(total), (EXTRA, 2 * lanes), 0)
        for side in range(2):
            target = (g0 * 2 + side) * 2 + cores[h]
            index = 2 * side + cores[h]
            columns = slice(side * lanes, (side + 1) * lanes)
            ob[index, 0:HD, :] = acc[:, columns].astype(BF16)
            ob[index, HD : HD + EXTRA, :] = extra[:, columns].astype(BF16)

            @pl.when(target != ctx)
            def _():
                pltpu.make_async_remote_copy(
                    src_ref=ob.at[index],
                    dst_ref=rb.at[seat],
                    send_sem=s_o_send,
                    recv_sem=s_o_recv,
                    device_id=(target, z),
                    device_id_type=MESH,
                ).start()

            @pl.when(target == ctx)
            def _():
                pltpu.make_async_copy(ob.at[index], rb.at[seat], s_o_recv).start()

    share_adapters()

    pltpu.make_async_copy(rb, rb, s_o_recv).wait()
    tops, totals = [], []
    for k in range(4):
        extra = rb[k, HD : HD + EXTRA, :].astype(F32)
        tops.append(extra[0:1] + extra[1:2] + extra[2:3])
        totals.append(extra[3:4] + extra[4:5] + extra[5:6])
    top = functools.reduce(jnp.maximum, tops)
    acc = jnp.zeros((HD, lanes), F32)
    total = jnp.zeros((1, lanes), F32)
    for k in range(4):
        factor = jnp.exp2(tops[k] - top)
        acc = acc + factor * rb[k, 0:HD, :].astype(F32)
        total = total + factor * totals[k]
    extra = stacked(three(top) + three(total), (HD, lanes), 0)
    zs[...] = jnp.concatenate(
        [acc.T.reshape(n_row, 8, HD), extra.T.reshape(n_row, 8, HD)], axis=1
    ).astype(BF16)

    def send_z(i, carry):
        step = n_row // 2 + jnp.where(i % 2 == 0, -(i // 2), i // 2)
        pltpu.make_async_remote_copy(
            src_ref=zs.at[step],
            dst_ref=zr.at[z],
            send_sem=s_z_send,
            recv_sem=s_z_recv,
            device_id=(ctx, lax.rem(z + step, n_row)),
            device_id_type=MESH,
        ).start()
        return carry

    lax.fori_loop(1, n_row, send_z, 0)
    zr[z] = zs[0]

    part = sr.at[0 : n_ctx - 1]
    pltpu.make_async_copy(part, part, s_s_recv).wait()
    near = merged(sr[...])

    adapters_here()
    rank = down_hbm.shape[1]
    width = n_row * rank // 2
    dt[...] = ad[:, :, 0].reshape(n_row * rank, 2 * HD).T
    row = lax.broadcasted_iota(jnp.int32, (2 * OWN, width), 0)
    col = lax.broadcasted_iota(jnp.int32, (2 * OWN, width), 1)
    wanted = jnp.zeros((2 * OWN, width), jnp.int32)
    for k in range(OWN):
        adapter = idx_ref[0, k]
        wanted = jnp.where(
            lax.rem(row, OWN) == k, (adapter % NEAR) * groups + adapter // NEAR, wanted
        )
    mine = wanted == col // rank + (n_row // 2) * (row // OWN)
    seated = col // rank == lax.rem(row, OWN)

    def fold(value):
        shift = width // 2
        while shift >= rank:
            value = value + pltpu.roll(value, shift, 1)
            shift //= 2
        return value


    part = zr.at[0 : n_row - 1]
    pltpu.make_async_copy(part, part, s_z_recv).wait()
    far = merged(zr[...])
    top = jnp.maximum(near[0], far[0])
    parts = [jnp.exp2(near[0] - top), jnp.exp2(far[0] - top)]
    total = parts[0] * near[1] + parts[1] * far[1]
    acc = parts[0] * near[2] + parts[1] * far[2]
    attended = (acc / total).astype(BF16).astype(F32)
    attended = jnp.concatenate([attended[0:OWN], attended[OWN : 2 * OWN]], axis=1)
    out_ref[0] = attended.astype(BF16)

    twice = jnp.concatenate([attended, attended], axis=0).astype(BF16)
    low = jnp.dot(twice, dt[...], preferred_element_type=F32)
    low = jnp.where(row < OWN, low[:, :width], low[:, width:])
    low = fold(jnp.where(mine, low, 0.0))
    ls[...] = jnp.sum(jnp.where(seated, low, 0.0), axis=0, keepdims=True)

    def send_l(d, carry):
        pltpu.make_async_remote_copy(
            src_ref=ls,
            dst_ref=lr.at[ctx],
            send_sem=s_l_send,
            recv_sem=s_l_recv,
            device_id=(lax.rem(ctx + d, n_ctx), z),
            device_id_type=MESH,
        ).start()
        return carry

    lax.fori_loop(1, n_ctx, send_l, 0)
    lr[ctx] = ls[...]
    pltpu.make_async_copy(lr.at[0 : n_ctx - 1], lr.at[0 : n_ctx - 1], s_l_recv).wait()
    low = jnp.broadcast_to(jnp.sum(lr[...], axis=0), (2 * OWN, width))
    low = jnp.where(mine, fold(jnp.where(seated, low, 0.0)), 0.0).astype(BF16)
    up = ad[:, :, 1].reshape(n_row * rank, 2 * HD)
    first = jnp.dot(low, up[:width], preferred_element_type=F32)
    second = jnp.dot(low, up[width:], preferred_element_type=F32)
    delta = first[0:OWN] + second[OWN : 2 * OWN]
    out_ref[1] = (attended + delta.astype(BF16).astype(F32)).astype(BF16)

    finish(99)


def body(n_ctx, n_row, queries, prefix, suffix, lengths, adapters, down, up):
    chips = n_ctx // 2
    pairs = chips // 2
    breadth = chips // COLUMN
    lanes = n_row * 8
    pd = prefix.shape[1]
    sd = suffix.shape[1] * suffix.shape[2]
    width = prefix.shape[2]
    rank = down.shape[2]
    suffix = suffix.reshape(2, sd, width)
    adapters = adapters.T
    down = jnp.transpose(down, (0, 2, 1))
    hbm = pl.BlockSpec(memory_space=pltpu.HBM)
    vmem = pl.BlockSpec(memory_space=pltpu.VMEM)
    dma = pltpu.SemaphoreType.DMA
    both = pl.pallas_call(
        functools.partial(kernel, n_ctx, n_row),
        out_shape=jax.ShapeDtypeStruct((2, OWN, 2 * HD), BF16),
        in_specs=[hbm] * 7,
        out_specs=vmem,
        scratch_shapes=[
            pltpu.SMEM(lengths.shape, jnp.int32),
            pltpu.SMEM(adapters.shape, jnp.int32),
            pltpu.VMEM(queries.shape, BF16),
            pltpu.VMEM((pairs * GROUP * OWN, HD), F32),
            pltpu.VMEM((VEC, HD), F32),
            pltpu.VMEM(suffix.shape, BF16),
            pltpu.VMEM((n_ctx, 16, HD), BF16),
            pltpu.VMEM((n_ctx, 16, HD), BF16),
            pltpu.VMEM((2, 2 * breadth, pd, HD), BF16),
            pltpu.VMEM((breadth, HD, 2 * pd), BF16),
            pltpu.VMEM((2, n_row * VEC, HD), BF16),
            pltpu.VMEM((2, breadth, 2 * pd, 2 * lanes), F32),
            pltpu.VMEM((4, HD + EXTRA, lanes), BF16),
            pltpu.VMEM((4, HD + EXTRA, lanes), BF16),
            pltpu.VMEM((n_row, 16, HD), BF16),
            pltpu.VMEM((n_row, 16, HD), BF16),
            pltpu.VMEM((NEAR, n_row // NEAR, 2, rank, 2 * HD), BF16),
            pltpu.VMEM((2 * HD, n_row * rank), BF16),
            pltpu.VMEM((1, n_row * rank // 2), F32),
            pltpu.VMEM((n_ctx, 1, n_row * rank // 2), F32),
            dma,
            dma,
            dma((4,)),
            dma((3,)),
            dma((3,)),
            dma((2,)),
            dma((2, 3)),
            dma,
            dma((2, 2 * breadth)),
            dma,
            dma,
            dma,
            dma,
            dma,
            dma,
            dma,
            dma,
        ],
        compiler_params=pltpu.CompilerParams(
            collective_id=0, has_side_effects=True, vmem_limit_bytes=64 * 1024 * 1024
        ),
        name="decode_attention",
    )(queries, prefix, suffix, lengths, adapters, down, up)
    return both[0], both[1]


def solution(mesh):
    return jax.shard_map(
        functools.partial(body, mesh.shape["ctx"], mesh.shape["row"]),
        mesh=mesh,
        in_specs=(
            P("row", None),
            P(None, ("ctx", "row"), None),
            P(None, "row", "ctx", None),
            P("row"),
            P("row", None),
            P("row", "ctx", None),
            P("row", None, "ctx"),
        ),
        out_specs=(P("row", "ctx"), P("row", "ctx")),
        check_vma=False,
    )
```

```python
import functools
import math

import jax
import jax.numpy as jnp
from jax import lax
from jax.experimental import pallas as pl
from jax.experimental.pallas import tpu as pltpu
from jax.sharding import PartitionSpec as P

HD = 128
GROUP = 8
OWN = 4
VEC = 16
EXTRA = 16
COLUMN = 4
NEAR = 4
MESH = pl.DeviceIdType.MESH
F32 = jnp.float32
BF16 = jnp.bfloat16


def three(value):
    high = value.astype(BF16).astype(F32)
    rest = value - high
    middle = rest.astype(BF16).astype(F32)
    return [high, middle, rest - middle]


def stacked(parts, shape, axis):
    at = lax.broadcasted_iota(jnp.int32, shape, axis)
    out = jnp.zeros(shape, F32)
    for index, part in enumerate(parts):
        out = jnp.where(at == index, jnp.broadcast_to(part, shape), out)
    return out


def contract_last(a, b):
    return lax.dot_general(a, b, (((1,), (1,)), ((), ())), preferred_element_type=F32)


def merged(arrived):
    count = arrived.shape[0]
    wide = arrived.astype(F32)
    extra = wide[:, 8:16, :].reshape(count * 8, HD).astype(BF16)
    row = lax.broadcasted_iota(jnp.int32, (HD, 2 * HD), 0)
    col = lax.broadcasted_iota(jnp.int32, (HD, 2 * HD), 1)
    pick = jnp.where(row // 3 == col // HD, 1.0, 0.0).astype(BF16)
    spread = jnp.dot(extra, pick, preferred_element_type=F32)
    tops = spread[:, :HD].reshape(count, 8, HD)
    totals = spread[:, HD:].reshape(count, 8, HD)
    top = jnp.max(tops, axis=0)
    factor = jnp.exp2(tops - top[None])
    return top, jnp.sum(factor * totals, axis=0), jnp.sum(factor * wide[:, 0:8, :], axis=0)


def kernel(
    n_ctx,
    n_row,
    q_hbm,
    kv_hbm,
    suf_hbm,
    len_hbm,
    idx_hbm,
    down_hbm,
    up_hbm,
    out_ref,
    len_ref,
    idx_ref,
    qv,
    qall,
    qown,
    sufv,
    sx,
    sr,
    kvb,
    vt,
    qb,
    sc,
    ob,
    rb,
    zs,
    zr,
    ad,
    dt,
    ls,
    lr,
    s_q,
    s_suf,
    s_ad_loc,
    s_ad_send,
    s_ad_recv,
    s_a_send,
    s_a_recv,
    s_kv_send,
    s_kv_recv,
    s_s_send,
    s_s_recv,
    s_o_send,
    s_o_recv,
    s_z_send,
    s_z_recv,
    s_l_send,
    s_l_recv,
):
    chips = n_ctx // 2
    pairs = chips // 2
    breadth = chips // COLUMN
    lanes = n_row * 8
    pd = kv_hbm.shape[1]
    sd = suf_hbm.shape[1]
    spos = sd // OWN
    scale = HD**-0.5 * math.log2(math.e)

    ctx = lax.axis_index("ctx")
    z = lax.axis_index("row")
    c = lax.rem(ctx, 2)
    groups = n_row // NEAR
    zl = lax.rem(z, NEAR)
    zh = z // NEAR
    chip = ctx // 2
    x = chip // COLUMN
    y = lax.rem(chip, COLUMN)
    sib = ctx + 1 - 2 * c

    owns = y % 2 == x // 2
    lead = jnp.where(owns, x, (x + 2) % COLUMN)
    g0 = 2 * lead + jnp.where(owns, y, (y + 2) % COLUMN) // 2
    seat = 2 * jnp.where(owns, 0, 1) + c

    def across(i, count):
        return count // 2 + jnp.where(i % 2 == 0, -(i // 2), i // 2)

    barrier = pltpu.get_barrier_semaphore()

    def greet_line(d, carry):
        target = lax.rem(z + d + jnp.where(d < NEAR, n_row - NEAR, n_row - NEAR + 1), n_row)
        for there in (ctx, sib):
            pl.semaphore_signal(barrier, 1, device_id=(there, target), device_id_type=MESH)
        return carry

    def greet_plane(d, carry):
        pl.semaphore_signal(
            barrier,
            1,
            device_id=(lax.rem(ctx + across(d, n_ctx), n_ctx), z),
            device_id_type=MESH,
        )
        return carry

    lax.fori_loop(0, 2 * NEAR, greet_line, 0)
    lax.fori_loop(1, n_ctx, greet_plane, 0)

    q_copy = pltpu.make_async_copy(q_hbm, qv, s_q)
    q_copy.start()
    suf_copy = pltpu.make_async_copy(suf_hbm, sufv, s_suf)
    suf_copy.start()
    ad_loc = [
        pltpu.make_async_copy(down_hbm.at[0], ad.at[zl, zh, 0], s_ad_loc.at[0]),
        pltpu.make_async_copy(up_hbm.at[0], ad.at[zl, zh, 1], s_ad_loc.at[1]),
    ]
    ad_loc.append(pltpu.make_async_copy(len_hbm, len_ref, s_ad_loc.at[2]))
    ad_loc.append(pltpu.make_async_copy(idx_hbm, idx_ref, s_ad_loc.at[3]))
    for copy in ad_loc:
        copy.start()

    q_copy.wait()
    queries = qv[...].astype(F32)
    for head in range(pairs * GROUP):
        qall[head * OWN : (head + 1) * OWN, :] = queries[:, head * HD : (head + 1) * HD]
    for side in range(2):
        start = pl.multiple_of(g0 * (GROUP * OWN) + side * VEC + 8 * c, 8)
        qown[side * 8 : (side + 1) * 8, :] = qall[pl.ds(start, 8), :]
    qb[c, 0:VEC, :] = qown[...].astype(BF16)

    pl.semaphore_wait(barrier, n_ctx - 1 + 4 * NEAR)

    def send_q(first, count, place, there, step, sems):
        pltpu.make_async_remote_copy(
            src_ref=qb.at[c, first * VEC : (first + count) * VEC],
            dst_ref=qb.at[c, place * VEC : (place + count) * VEC],
            send_sem=s_a_send.at[sems // 2],
            recv_sem=s_a_recv.at[c, sems],
            device_id=(there, lax.rem(z + step + n_row, n_row)),
            device_id_type=MESH,
        ).start()

    def wait_q(core, kind, count):
        part = qb.at[0, 0 : count * VEC]
        pltpu.make_async_copy(part, part, s_a_recv.at[core, kind]).wait()

    for d in range(NEAR, 0, -1):
        for there in (ctx, sib):
            send_q(0, 1, n_row - d, there, d, 0)
        if d < NEAR:
            for there in (ctx, sib):
                send_q(0, 1, d, there, -d, 1)
    send_q(0, 1, 0, sib, 0, 1)

    def send_far(block, step, kind):
        pltpu.make_async_remote_copy(
            src_ref=ad.at[zl, block],
            dst_ref=ad.at[zl, block],
            send_sem=s_ad_send.at[kind],
            recv_sem=s_ad_recv.at[kind],
            device_id=(ctx, lax.rem(z + step + n_row, n_row)),
            device_id_type=MESH,
        ).start()

    def pass_adapters():
        part = ad.at[0, 0:2]
        pltpu.make_async_copy(part, part, s_ad_recv.at[0]).wait()
        send_far(lax.rem(zh + groups - 1, groups), NEAR, 1)

    def share_adapters():
        part = ad.at[0, 0]
        pltpu.make_async_copy(part, part, s_ad_recv.at[1]).wait()
        for d in (1, n_row - 1, 2):
            pltpu.make_async_remote_copy(
                src_ref=ad.at[zl],
                dst_ref=ad.at[zl],
                send_sem=s_ad_send.at[2],
                recv_sem=s_ad_recv.at[2],
                device_id=(ctx, lax.rem(z + d, n_row)),
                device_id_type=MESH,
            ).start()

    for copy in ad_loc:
        copy.wait()
    send_far(zh, NEAR, 0)
    send_far(zh, -NEAR, 0)

    def place_kv(i, g):
        home_x = g // 2
        home_y = 2 * (g % 2) + g // 4
        dx = (x - home_x + COLUMN) % COLUMN
        dy = (y - home_y + COLUMN) % COLUMN
        far = jnp.where(dx == 3, 1, dx) + jnp.where(dy == 3, 1, dy)
        level = jnp.where(dx == dy, 1, jnp.where(dx == 2 * (g % 2), 1, 0))
        level = jnp.where(jnp.logical_and(dx % 2 == 1, dx != dy), 0, level)
        stay = jnp.where(far == 2, level, jnp.where(far < 2, 1, 0))
        dx = (dx + 2 * (1 - stay)) % COLUMN
        dy = (dy + 2 * (1 - stay)) % COLUMN
        target_x = (home_x + 2 * (1 - stay)) % COLUMN
        target_y = (home_y + 2 * (1 - stay)) % COLUMN
        one = jnp.where(dy == 0, (dx + 1) // 2, jnp.where(dy == 1, 3, 4))
        two = jnp.where(dx % 2 == 1, 5 + dx // 2, 7)
        near = jnp.logical_or(dx % 2 == 0, dy % 2 == 0)
        near = jnp.logical_and(near, jnp.logical_and(dx != 2, dy != 2))
        slot = jnp.where(near, one, two)
        columns = pl.ds(pl.multiple_of(g * HD, HD), HD)
        return target_x * COLUMN + target_y, slot, kv_hbm.at[i, :, columns]

    for i in range(2):

        def send_kv(d, carry):
            target, slot, part = place_kv(i, lax.rem(g0 + d, pairs))
            pltpu.make_async_remote_copy(
                src_ref=part,
                dst_ref=kvb.at[i, slot],
                send_sem=s_kv_send,
                recv_sem=s_kv_recv.at[i, slot],
                device_id=(target * 2 + c, z),
                device_id_type=MESH,
            ).start()
            return carry

        lax.fori_loop(1, pairs, send_kv, 0)
        _, slot, part = place_kv(i, g0)
        pltpu.make_async_copy(part, kvb.at[i, slot], s_kv_recv.at[i, slot]).start()

    wait_q(c, 0, NEAR)
    for there in (ctx, sib):
        send_q(n_row - NEAR, NEAR, n_row - 2 * NEAR, there, NEAR, 2)
    wait_q(c, 1, NEAR - 1)
    for there in (ctx, sib):
        send_q(0, NEAR, NEAR, there, -NEAR, 2)

    suf_copy.wait()
    at = lax.broadcasted_iota(jnp.int32, (GROUP * OWN, sd), 1)
    row = lax.broadcasted_iota(jnp.int32, (GROUP * OWN, sd), 0)
    owner = at // spos
    live = jnp.zeros((GROUP * OWN, sd), jnp.int32)
    for k in range(OWN):
        live = jnp.where(owner == k, len_ref[k], live)
    valid = (lax.rem(row, OWN) == owner) & (ctx * spos + lax.rem(at, spos) < live)
    for g in range(pairs):
        vectors = qall[g * GROUP * OWN : (g + 1) * GROUP * OWN, :].astype(BF16)
        scores = contract_last(vectors, sufv[0, :, g * HD : (g + 1) * HD]) * scale
        scores = jnp.where(valid, scores, -1e30)
        top = jnp.max(scores, axis=1, keepdims=True)
        weights = jnp.exp2(scores - top)
        total = jnp.sum(weights, axis=1, keepdims=True)
        out = jnp.dot(
            weights.astype(BF16),
            sufv[1, :, g * HD : (g + 1) * HD],
            preferred_element_type=F32,
        )
        extra = stacked(three(top) + three(total), (GROUP * OWN, HD), 1)
        sx[4 * g : 4 * g + 4] = jnp.concatenate(
            [out.reshape(4, 8, HD), extra.reshape(4, 8, HD)], axis=1
        ).astype(BF16)

    def adapters_here():
        part = ad.at[0 : NEAR - 1]
        pltpu.make_async_copy(part, part, s_ad_recv.at[2]).wait()

    def finish(k):
        part = ad.at[0, 0:2]
        pltpu.make_async_copy(part, part, s_ad_send.at[0]).wait()
        part = ad.at[0, 0]
        pltpu.make_async_copy(part, part, s_ad_send.at[1]).wait()
        part = ad.at[0 : NEAR - 1]
        pltpu.make_async_copy(part, part, s_ad_send.at[2]).wait()
        part = qb.at[0, 0 : (4 * NEAR - 1) * VEC]
        pltpu.make_async_copy(part, part, s_a_send.at[0]).wait()
        part = qb.at[0, 0 : 4 * NEAR * VEC]
        pltpu.make_async_copy(part, part, s_a_send.at[1]).wait()
        part = kvb.at[:, 0 : pairs - 1]
        pltpu.make_async_copy(part, part, s_kv_send).wait()
        part = sx.at[0 : n_ctx - 1]
        pltpu.make_async_copy(part, part, s_s_send).wait()
        part = ob.at[0:3]

        @pl.when(owns)
        def _():
            pltpu.make_async_copy(part, part, s_o_send).wait()

        @pl.when(jnp.logical_not(owns))
        def _():
            pltpu.make_async_copy(ob, ob, s_o_send).wait()

        part = zs.at[0 : n_row - 1]
        pltpu.make_async_copy(part, part, s_z_send).wait()
        part = lr.at[0 : n_ctx - 1]
        pltpu.make_async_copy(part, part, s_l_send).wait()

    wait_q(c, 2, 2 * NEAR)
    pass_adapters()

    def vectors_of(core):
        wide = qb[core].astype(F32).reshape(n_row, 2, 8, HD)
        return jnp.concatenate(
            [wide[:, side].reshape(lanes, HD) for side in range(2)], axis=0
        ).astype(BF16)

    def arrive(i, j):
        for side in range(2):
            slot = 2 * j + side
            pltpu.make_async_copy(
                kvb.at[i, slot], kvb.at[i, slot], s_kv_recv.at[i, slot]
            ).wait()

    cores = (c, 1 - c)
    tops = []
    for h in range(2):
        if h == 1:
            wait_q(1 - c, 0, NEAR)
            wait_q(1 - c, 1, NEAR)
            wait_q(1 - c, 2, 2 * NEAR)
        vectors = vectors_of(cores[h])
        top = None
        for j in range(breadth):
            if h == 0:
                arrive(0, j)
            keys = kvb[0, 2 * j : 2 * j + 2].reshape(2 * pd, HD)
            scores = contract_last(keys, vectors) * scale
            sc[h, j] = scores
            best = jnp.max(scores, axis=0, keepdims=True)
            top = best if top is None else jnp.maximum(top, best)
        tops.append(top)
    for j in range(breadth):
        arrive(1, j)
        vt[j] = kvb[1, 2 * j : 2 * j + 2].reshape(2 * pd, HD).T

    for h in range(2):
        total = jnp.zeros((1, 2 * lanes), F32)
        acc = jnp.zeros((HD, 2 * lanes), F32)
        for j in range(breadth):
            weights = jnp.exp2(sc[h, j] - tops[h])
            total = total + jnp.sum(weights, axis=0, keepdims=True)
            acc = acc + jnp.dot(vt[j], weights.astype(BF16), preferred_element_type=F32)
        extra = stacked(three(tops[h]) + three(total), (EXTRA, 2 * lanes), 0)
        for side in range(2):
            target = (g0 * 2 + side) * 2 + cores[h]
            index = 2 * side + cores[h]
            columns = slice(side * lanes, (side + 1) * lanes)
            ob[index, 0:HD, :] = acc[:, columns].astype(BF16)
            ob[index, HD : HD + EXTRA, :] = extra[:, columns].astype(BF16)

            @pl.when(target != ctx)
            def _():
                pltpu.make_async_remote_copy(
                    src_ref=ob.at[index],
                    dst_ref=rb.at[seat],
                    send_sem=s_o_send,
                    recv_sem=s_o_recv,
                    device_id=(target, z),
                    device_id_type=MESH,
                ).start()

            @pl.when(target == ctx)
            def _():
                pltpu.make_async_copy(ob.at[index], rb.at[seat], s_o_recv).start()

    share_adapters()

    pltpu.make_async_copy(rb, rb, s_o_recv).wait()
    tops, totals = [], []
    for k in range(4):
        extra = rb[k, HD : HD + EXTRA, :].astype(F32)
        tops.append(extra[0:1] + extra[1:2] + extra[2:3])
        totals.append(extra[3:4] + extra[4:5] + extra[5:6])
    top = functools.reduce(jnp.maximum, tops)
    acc = jnp.zeros((HD, lanes), F32)
    total = jnp.zeros((1, lanes), F32)
    for k in range(4):
        factor = jnp.exp2(tops[k] - top)
        acc = acc + factor * rb[k, 0:HD, :].astype(F32)
        total = total + factor * totals[k]
    extra = stacked(three(top) + three(total), (HD, lanes), 0)
    zs[...] = jnp.concatenate(
        [acc.T.reshape(n_row, 8, HD), extra.T.reshape(n_row, 8, HD)], axis=1
    ).astype(BF16)

    def send_z(i, carry):
        target = i - 1 + jnp.where(i > z, 1, 0)
        step = lax.rem(target - z + n_row, n_row)
        pltpu.make_async_remote_copy(
            src_ref=zs.at[step],
            dst_ref=zr.at[z],
            send_sem=s_z_send,
            recv_sem=s_z_recv,
            device_id=(ctx, target),
            device_id_type=MESH,
        ).start()
        return carry

    lax.fori_loop(1, n_row, send_z, 0)
    zr[z] = zs[0]
    def send_s(d, carry):
        target = lax.rem(ctx + d, n_ctx)
        pltpu.make_async_remote_copy(
            src_ref=sx.at[target],
            dst_ref=sr.at[ctx],
            send_sem=s_s_send,
            recv_sem=s_s_recv,
            device_id=(target, z),
            device_id_type=MESH,
        ).start()
        return carry

    lax.fori_loop(1, n_ctx, send_s, 0)
    sr[ctx] = sx[ctx]


    part = sr.at[0 : n_ctx - 1]
    pltpu.make_async_copy(part, part, s_s_recv).wait()
    near = merged(sr[...])

    adapters_here()
    rank = down_hbm.shape[1]
    width = n_row * rank // 2
    dt[...] = ad[:, :, 0].reshape(n_row * rank, 2 * HD).T
    row = lax.broadcasted_iota(jnp.int32, (2 * OWN, width), 0)
    col = lax.broadcasted_iota(jnp.int32, (2 * OWN, width), 1)
    wanted = jnp.zeros((2 * OWN, width), jnp.int32)
    for k in range(OWN):
        adapter = idx_ref[0, k]
        wanted = jnp.where(
            lax.rem(row, OWN) == k, (adapter % NEAR) * groups + adapter // NEAR, wanted
        )
    mine = wanted == col // rank + (n_row // 2) * (row // OWN)
    seated = col // rank == lax.rem(row, OWN)

    def fold(value):
        shift = width // 2
        while shift >= rank:
            value = value + pltpu.roll(value, shift, 1)
            shift //= 2
        return value


    part = zr.at[0 : n_row - 1]
    pltpu.make_async_copy(part, part, s_z_recv).wait()
    far = merged(zr[...])
    top = jnp.maximum(near[0], far[0])
    parts = [jnp.exp2(near[0] - top), jnp.exp2(far[0] - top)]
    total = parts[0] * near[1] + parts[1] * far[1]
    acc = parts[0] * near[2] + parts[1] * far[2]
    attended = (acc / total).astype(BF16).astype(F32)
    attended = jnp.concatenate([attended[0:OWN], attended[OWN : 2 * OWN]], axis=1)
    out_ref[0] = attended.astype(BF16)

    twice = jnp.concatenate([attended, attended], axis=0).astype(BF16)
    low = jnp.dot(twice, dt[...], preferred_element_type=F32)
    low = jnp.where(row < OWN, low[:, :width], low[:, width:])
    low = fold(jnp.where(mine, low, 0.0))
    ls[...] = jnp.sum(jnp.where(seated, low, 0.0), axis=0, keepdims=True)

    def send_l(d, carry):
        pltpu.make_async_remote_copy(
            src_ref=ls,
            dst_ref=lr.at[ctx],
            send_sem=s_l_send,
            recv_sem=s_l_recv,
            device_id=(lax.rem(ctx + across(d, n_ctx), n_ctx), z),
            device_id_type=MESH,
        ).start()
        return carry

    lax.fori_loop(1, n_ctx, send_l, 0)
    lr[ctx] = ls[...]
    pltpu.make_async_copy(lr.at[0 : n_ctx - 1], lr.at[0 : n_ctx - 1], s_l_recv).wait()
    low = jnp.broadcast_to(jnp.sum(lr[...], axis=0), (2 * OWN, width))
    low = jnp.where(mine, fold(jnp.where(seated, low, 0.0)), 0.0).astype(BF16)
    up = ad[:, :, 1].reshape(n_row * rank, 2 * HD)
    first = jnp.dot(low, up[:width], preferred_element_type=F32)
    second = jnp.dot(low, up[width:], preferred_element_type=F32)
    delta = first[0:OWN] + second[OWN : 2 * OWN]
    out_ref[1] = (attended + delta.astype(BF16).astype(F32)).astype(BF16)

    finish(99)


def body(n_ctx, n_row, queries, prefix, suffix, lengths, adapters, down, up):
    chips = n_ctx // 2
    pairs = chips // 2
    breadth = chips // COLUMN
    lanes = n_row * 8
    pd = prefix.shape[1]
    sd = suffix.shape[1] * suffix.shape[2]
    width = prefix.shape[2]
    rank = down.shape[2]
    suffix = suffix.reshape(2, sd, width)
    adapters = adapters.T
    down = jnp.transpose(down, (0, 2, 1))
    hbm = pl.BlockSpec(memory_space=pltpu.HBM)
    vmem = pl.BlockSpec(memory_space=pltpu.VMEM)
    dma = pltpu.SemaphoreType.DMA
    both = pl.pallas_call(
        functools.partial(kernel, n_ctx, n_row),
        out_shape=jax.ShapeDtypeStruct((2, OWN, 2 * HD), BF16),
        in_specs=[hbm] * 7,
        out_specs=vmem,
        scratch_shapes=[
            pltpu.SMEM(lengths.shape, jnp.int32),
            pltpu.SMEM(adapters.shape, jnp.int32),
            pltpu.VMEM(queries.shape, BF16),
            pltpu.VMEM((pairs * GROUP * OWN, HD), F32),
            pltpu.VMEM((VEC, HD), F32),
            pltpu.VMEM(suffix.shape, BF16),
            pltpu.VMEM((n_ctx, 16, HD), BF16),
            pltpu.VMEM((n_ctx, 16, HD), BF16),
            pltpu.VMEM((2, 2 * breadth, pd, HD), BF16),
            pltpu.VMEM((breadth, HD, 2 * pd), BF16),
            pltpu.VMEM((2, n_row * VEC, HD), BF16),
            pltpu.VMEM((2, breadth, 2 * pd, 2 * lanes), F32),
            pltpu.VMEM((4, HD + EXTRA, lanes), BF16),
            pltpu.VMEM((4, HD + EXTRA, lanes), BF16),
            pltpu.VMEM((n_row, 16, HD), BF16),
            pltpu.VMEM((n_row, 16, HD), BF16),
            pltpu.VMEM((NEAR, n_row // NEAR, 2, rank, 2 * HD), BF16),
            pltpu.VMEM((2 * HD, n_row * rank), BF16),
            pltpu.VMEM((1, n_row * rank // 2), F32),
            pltpu.VMEM((n_ctx, 1, n_row * rank // 2), F32),
            dma,
            dma,
            dma((4,)),
            dma((3,)),
            dma((3,)),
            dma((2,)),
            dma((2, 3)),
            dma,
            dma((2, 2 * breadth)),
            dma,
            dma,
            dma,
            dma,
            dma,
            dma,
            dma,
            dma,
        ],
        compiler_params=pltpu.CompilerParams(
            collective_id=0, has_side_effects=True, vmem_limit_bytes=64 * 1024 * 1024
        ),
        name="decode_attention",
    )(queries, prefix, suffix, lengths, adapters, down, up)
    return both[0], both[1]


def solution(mesh):
    return jax.shard_map(
        functools.partial(body, mesh.shape["ctx"], mesh.shape["row"]),
        mesh=mesh,
        in_specs=(
            P("row", None),
            P(None, ("ctx", "row"), None),
            P(None, "row", "ctx", None),
            P("row"),
            P("row", None),
            P("row", "ctx", None),
            P("row", None, "ctx"),
        ),
        out_specs=(P("row", "ctx"), P("row", "ctx")),
        check_vma=False,
    )
```

```python
import functools
import math

import jax
import jax.numpy as jnp
from jax import lax
from jax.experimental import pallas as pl
from jax.experimental.pallas import tpu as pltpu
from jax.sharding import PartitionSpec as P

HD = 128
GROUP = 8
OWN = 4
VEC = 16
EXTRA = 16
COLUMN = 4
NEAR = 4
MESH = pl.DeviceIdType.MESH
F32 = jnp.float32
BF16 = jnp.bfloat16


def three(value):
    high = value.astype(BF16).astype(F32)
    rest = value - high
    middle = rest.astype(BF16).astype(F32)
    return [high, middle, rest - middle]


def stacked(parts, shape, axis):
    at = lax.broadcasted_iota(jnp.int32, shape, axis)
    out = jnp.zeros(shape, F32)
    for index, part in enumerate(parts):
        out = jnp.where(at == index, jnp.broadcast_to(part, shape), out)
    return out


def contract_last(a, b):
    return lax.dot_general(a, b, (((1,), (1,)), ((), ())), preferred_element_type=F32)


def merged(arrived):
    count = arrived.shape[0]
    wide = arrived.astype(F32)
    extra = wide[:, 8:16, :].reshape(count * 8, HD).astype(BF16)
    row = lax.broadcasted_iota(jnp.int32, (HD, 2 * HD), 0)
    col = lax.broadcasted_iota(jnp.int32, (HD, 2 * HD), 1)
    pick = jnp.where(row // 3 == col // HD, 1.0, 0.0).astype(BF16)
    spread = jnp.dot(extra, pick, preferred_element_type=F32)
    tops = spread[:, :HD].reshape(count, 8, HD)
    totals = spread[:, HD:].reshape(count, 8, HD)
    top = jnp.max(tops, axis=0)
    factor = jnp.exp2(tops - top[None])
    return top, jnp.sum(factor * totals, axis=0), jnp.sum(factor * wide[:, 0:8, :], axis=0)


def kernel(
    n_ctx,
    n_row,
    q_hbm,
    kv_hbm,
    suf_hbm,
    len_hbm,
    idx_hbm,
    down_hbm,
    up_hbm,
    out_ref,
    len_ref,
    idx_ref,
    qv,
    qall,
    qown,
    sufv,
    sx,
    sr,
    kvb,
    vt,
    qb,
    sc,
    ob,
    rb,
    zs,
    zr,
    ad,
    dt,
    ls,
    lr,
    s_q,
    s_suf,
    s_ad_loc,
    s_ad_send,
    s_ad_recv,
    s_a_send,
    s_a_recv,
    s_kv_send,
    s_kv_recv,
    s_s_send,
    s_s_recv,
    s_o_send,
    s_o_recv,
    s_z_send,
    s_z_recv,
    s_l_send,
    s_l_recv,
):
    chips = n_ctx // 2
    pairs = chips // 2
    breadth = chips // COLUMN
    lanes = n_row * 8
    pd = kv_hbm.shape[1]
    sd = suf_hbm.shape[1]
    spos = sd // OWN
    scale = HD**-0.5 * math.log2(math.e)

    ctx = lax.axis_index("ctx")
    z = lax.axis_index("row")
    c = lax.rem(ctx, 2)
    groups = n_row // NEAR
    zl = lax.rem(z, NEAR)
    zh = z // NEAR
    chip = ctx // 2
    x = chip // COLUMN
    y = lax.rem(chip, COLUMN)
    sib = ctx + 1 - 2 * c

    owns = y % 2 == x // 2
    lead = jnp.where(owns, x, (x + 2) % COLUMN)
    g0 = 2 * lead + jnp.where(owns, y, (y + 2) % COLUMN) // 2
    seat = 2 * jnp.where(owns, 0, 1) + c

    def across(i, count):
        return count // 2 + jnp.where(i % 2 == 0, -(i // 2), i // 2)

    barrier = pltpu.get_barrier_semaphore()

    def greet_line(d, carry):
        target = lax.rem(z + d + jnp.where(d < NEAR, n_row - NEAR, n_row - NEAR + 1), n_row)
        for there in (ctx, sib):
            pl.semaphore_signal(barrier, 1, device_id=(there, target), device_id_type=MESH)
        return carry

    def greet_plane(d, carry):
        pl.semaphore_signal(
            barrier,
            1,
            device_id=(lax.rem(ctx + across(d, n_ctx), n_ctx), z),
            device_id_type=MESH,
        )
        return carry

    lax.fori_loop(1, n_ctx, greet_plane, 0)
    lax.fori_loop(0, 2 * NEAR, greet_line, 0)

    q_copy = pltpu.make_async_copy(q_hbm, qv, s_q)
    q_copy.start()
    suf_copy = pltpu.make_async_copy(suf_hbm, sufv, s_suf)
    suf_copy.start()
    ad_loc = [
        pltpu.make_async_copy(down_hbm.at[0], ad.at[zl, zh, 0], s_ad_loc.at[0]),
        pltpu.make_async_copy(up_hbm.at[0], ad.at[zl, zh, 1], s_ad_loc.at[1]),
    ]
    ad_loc.append(pltpu.make_async_copy(len_hbm, len_ref, s_ad_loc.at[2]))
    ad_loc.append(pltpu.make_async_copy(idx_hbm, idx_ref, s_ad_loc.at[3]))
    for copy in ad_loc:
        copy.start()

    q_copy.wait()
    queries = qv[...].astype(F32)
    for head in range(pairs * GROUP):
        qall[head * OWN : (head + 1) * OWN, :] = queries[:, head * HD : (head + 1) * HD]
    for side in range(2):
        start = pl.multiple_of(g0 * (GROUP * OWN) + side * VEC + 8 * c, 8)
        qown[side * 8 : (side + 1) * 8, :] = qall[pl.ds(start, 8), :]
    qb[c, 0:VEC, :] = qown[...].astype(BF16)

    pl.semaphore_wait(barrier, n_ctx - 1 + 4 * NEAR)

    def send_q(first, count, place, there, step, sems):
        pltpu.make_async_remote_copy(
            src_ref=qb.at[c, first * VEC : (first + count) * VEC],
            dst_ref=qb.at[c, place * VEC : (place + count) * VEC],
            send_sem=s_a_send.at[sems // 2],
            recv_sem=s_a_recv.at[c, sems],
            device_id=(there, lax.rem(z + step + n_row, n_row)),
            device_id_type=MESH,
        ).start()

    def wait_q(core, kind, count):
        part = qb.at[0, 0 : count * VEC]
        pltpu.make_async_copy(part, part, s_a_recv.at[core, kind]).wait()

    for d in range(NEAR, 0, -1):
        for there in (ctx, sib):
            send_q(0, 1, n_row - d, there, d, 0)
        if d < NEAR:
            for there in (ctx, sib):
                send_q(0, 1, d, there, -d, 1)
    send_q(0, 1, 0, sib, 0, 1)

    def send_far(block, step, kind):
        pltpu.make_async_remote_copy(
            src_ref=ad.at[zl, block],
            dst_ref=ad.at[zl, block],
            send_sem=s_ad_send.at[kind],
            recv_sem=s_ad_recv.at[kind],
            device_id=(ctx, lax.rem(z + step + n_row, n_row)),
            device_id_type=MESH,
        ).start()

    def pass_adapters():
        part = ad.at[0, 0:2]
        pltpu.make_async_copy(part, part, s_ad_recv.at[0]).wait()
        send_far(lax.rem(zh + groups - 1, groups), NEAR, 1)

    def share_adapters():
        part = ad.at[0, 0]
        pltpu.make_async_copy(part, part, s_ad_recv.at[1]).wait()
        for d in (1, n_row - 1, 2):
            pltpu.make_async_remote_copy(
                src_ref=ad.at[zl],
                dst_ref=ad.at[zl],
                send_sem=s_ad_send.at[2],
                recv_sem=s_ad_recv.at[2],
                device_id=(ctx, lax.rem(z + d, n_row)),
                device_id_type=MESH,
            ).start()

    for copy in ad_loc:
        copy.wait()
    send_far(zh, NEAR, 0)
    send_far(zh, -NEAR, 0)

    def place_kv(i, g):
        home_x = g // 2
        home_y = 2 * (g % 2) + g // 4
        dx = (x - home_x + COLUMN) % COLUMN
        dy = (y - home_y + COLUMN) % COLUMN
        far = jnp.where(dx == 3, 1, dx) + jnp.where(dy == 3, 1, dy)
        level = jnp.where(dx == dy, 1, jnp.where(dx == 2 * (g % 2), 1, 0))
        level = jnp.where(jnp.logical_and(dx % 2 == 1, dx != dy), 0, level)
        stay = jnp.where(far == 2, level, jnp.where(far < 2, 1, 0))
        dx = (dx + 2 * (1 - stay)) % COLUMN
        dy = (dy + 2 * (1 - stay)) % COLUMN
        target_x = (home_x + 2 * (1 - stay)) % COLUMN
        target_y = (home_y + 2 * (1 - stay)) % COLUMN
        one = jnp.where(dy == 0, (dx + 1) // 2, jnp.where(dy == 1, 3, 4))
        two = jnp.where(dx % 2 == 1, 5 + dx // 2, 7)
        near = jnp.logical_or(dx % 2 == 0, dy % 2 == 0)
        near = jnp.logical_and(near, jnp.logical_and(dx != 2, dy != 2))
        slot = jnp.where(near, one, two)
        columns = pl.ds(pl.multiple_of(g * HD, HD), HD)
        return target_x * COLUMN + target_y, slot, kv_hbm.at[i, :, columns]

    for i in range(2):

        def send_kv(d, carry):
            target, slot, part = place_kv(i, lax.rem(g0 + d, pairs))
            pltpu.make_async_remote_copy(
                src_ref=part,
                dst_ref=kvb.at[i, slot],
                send_sem=s_kv_send,
                recv_sem=s_kv_recv.at[i, slot],
                device_id=(target * 2 + c, z),
                device_id_type=MESH,
            ).start()
            return carry

        lax.fori_loop(1, pairs, send_kv, 0)
        _, slot, part = place_kv(i, g0)
        pltpu.make_async_copy(part, kvb.at[i, slot], s_kv_recv.at[i, slot]).start()

    wait_q(c, 0, NEAR)
    for there in (ctx, sib):
        send_q(n_row - NEAR, NEAR, n_row - 2 * NEAR, there, NEAR, 2)
    wait_q(c, 1, NEAR - 1)
    for there in (ctx, sib):
        send_q(0, NEAR, NEAR, there, -NEAR, 2)

    pass_adapters()

    suf_copy.wait()
    at = lax.broadcasted_iota(jnp.int32, (GROUP * OWN, sd), 1)
    row = lax.broadcasted_iota(jnp.int32, (GROUP * OWN, sd), 0)
    owner = at // spos
    live = jnp.zeros((GROUP * OWN, sd), jnp.int32)
    for k in range(OWN):
        live = jnp.where(owner == k, len_ref[k], live)
    valid = (lax.rem(row, OWN) == owner) & (ctx * spos + lax.rem(at, spos) < live)
    for g in range(pairs):
        vectors = qall[g * GROUP * OWN : (g + 1) * GROUP * OWN, :].astype(BF16)
        scores = contract_last(vectors, sufv[0, :, g * HD : (g + 1) * HD]) * scale
        scores = jnp.where(valid, scores, -1e30)
        top = jnp.max(scores, axis=1, keepdims=True)
        weights = jnp.exp2(scores - top)
        total = jnp.sum(weights, axis=1, keepdims=True)
        out = jnp.dot(
            weights.astype(BF16),
            sufv[1, :, g * HD : (g + 1) * HD],
            preferred_element_type=F32,
        )
        extra = stacked(three(top) + three(total), (GROUP * OWN, HD), 1)
        sx[4 * g : 4 * g + 4] = jnp.concatenate(
            [out.reshape(4, 8, HD), extra.reshape(4, 8, HD)], axis=1
        ).astype(BF16)

    def adapters_here():
        part = ad.at[0 : NEAR - 1]
        pltpu.make_async_copy(part, part, s_ad_recv.at[2]).wait()

    def finish(k):
        part = ad.at[0, 0:2]
        pltpu.make_async_copy(part, part, s_ad_send.at[0]).wait()
        part = ad.at[0, 0]
        pltpu.make_async_copy(part, part, s_ad_send.at[1]).wait()
        part = ad.at[0 : NEAR - 1]
        pltpu.make_async_copy(part, part, s_ad_send.at[2]).wait()
        part = qb.at[0, 0 : (4 * NEAR - 1) * VEC]
        pltpu.make_async_copy(part, part, s_a_send.at[0]).wait()
        part = qb.at[0, 0 : 4 * NEAR * VEC]
        pltpu.make_async_copy(part, part, s_a_send.at[1]).wait()
        part = kvb.at[:, 0 : pairs - 1]
        pltpu.make_async_copy(part, part, s_kv_send).wait()
        part = sx.at[0 : n_ctx - 1]
        pltpu.make_async_copy(part, part, s_s_send).wait()
        part = ob.at[0:3]

        @pl.when(owns)
        def _():
            pltpu.make_async_copy(part, part, s_o_send).wait()

        @pl.when(jnp.logical_not(owns))
        def _():
            pltpu.make_async_copy(ob, ob, s_o_send).wait()

        part = zs.at[0 : n_row - 1]
        pltpu.make_async_copy(part, part, s_z_send).wait()
        part = lr.at[0 : n_ctx - 1]
        pltpu.make_async_copy(part, part, s_l_send).wait()

    wait_q(c, 2, 2 * NEAR)

    def vectors_of(core):
        wide = qb[core].astype(F32).reshape(n_row, 2, 8, HD)
        return jnp.concatenate(
            [wide[:, side].reshape(lanes, HD) for side in range(2)], axis=0
        ).astype(BF16)

    def arrive(i, j):
        for side in range(2):
            slot = 2 * j + side
            pltpu.make_async_copy(
                kvb.at[i, slot], kvb.at[i, slot], s_kv_recv.at[i, slot]
            ).wait()

    cores = (c, 1 - c)
    for h in range(2):
        if h == 1:
            wait_q(1 - c, 0, NEAR)
            wait_q(1 - c, 1, NEAR)
            wait_q(1 - c, 2, 2 * NEAR)
        vectors = vectors_of(cores[h])
        top = None
        for j in range(breadth):
            if h == 0:
                arrive(0, j)
            keys = kvb[0, 2 * j : 2 * j + 2].reshape(2 * pd, HD)
            scores = contract_last(keys, vectors) * scale
            sc[h, j] = scores
            best = jnp.max(scores, axis=0, keepdims=True)
            top = best if top is None else jnp.maximum(top, best)
        total = jnp.zeros((1, 2 * lanes), F32)
        acc = jnp.zeros((HD, 2 * lanes), F32)
        for j in range(breadth):
            if h == 0:
                arrive(1, j)
                vt[j] = kvb[1, 2 * j : 2 * j + 2].reshape(2 * pd, HD).T
            weights = jnp.exp2(sc[h, j] - top)
            total = total + jnp.sum(weights, axis=0, keepdims=True)
            acc = acc + jnp.dot(vt[j], weights.astype(BF16), preferred_element_type=F32)
        extra = stacked(three(top) + three(total), (EXTRA, 2 * lanes), 0)
        for side in range(2):
            target = (g0 * 2 + side) * 2 + cores[h]
            index = 2 * side + cores[h]
            columns = slice(side * lanes, (side + 1) * lanes)
            ob[index, 0:HD, :] = acc[:, columns].astype(BF16)
            ob[index, HD : HD + EXTRA, :] = extra[:, columns].astype(BF16)

            @pl.when(target != ctx)
            def _():
                pltpu.make_async_remote_copy(
                    src_ref=ob.at[index],
                    dst_ref=rb.at[seat],
                    send_sem=s_o_send,
                    recv_sem=s_o_recv,
                    device_id=(target, z),
                    device_id_type=MESH,
                ).start()

            @pl.when(target == ctx)
            def _():
                pltpu.make_async_copy(ob.at[index], rb.at[seat], s_o_recv).start()

    share_adapters()

    pltpu.make_async_copy(rb, rb, s_o_recv).wait()
    tops, totals = [], []
    for k in range(4):
        extra = rb[k, HD : HD + EXTRA, :].astype(F32)
        tops.append(extra[0:1] + extra[1:2] + extra[2:3])
        totals.append(extra[3:4] + extra[4:5] + extra[5:6])
    top = functools.reduce(jnp.maximum, tops)
    acc = jnp.zeros((HD, lanes), F32)
    total = jnp.zeros((1, lanes), F32)
    for k in range(4):
        factor = jnp.exp2(tops[k] - top)
        acc = acc + factor * rb[k, 0:HD, :].astype(F32)
        total = total + factor * totals[k]
    extra = stacked(three(top) + three(total), (HD, lanes), 0)
    zs[...] = jnp.concatenate(
        [acc.T.reshape(n_row, 8, HD), extra.T.reshape(n_row, 8, HD)], axis=1
    ).astype(BF16)

    def send_z(i, carry):
        target = i - 1 + jnp.where(i > z, 1, 0)
        step = lax.rem(target - z + n_row, n_row)
        pltpu.make_async_remote_copy(
            src_ref=zs.at[step],
            dst_ref=zr.at[z],
            send_sem=s_z_send,
            recv_sem=s_z_recv,
            device_id=(ctx, target),
            device_id_type=MESH,
        ).start()
        return carry

    lax.fori_loop(1, n_row, send_z, 0)
    zr[z] = zs[0]
    def send_s(d, carry):
        target = lax.rem(ctx + d, n_ctx)
        pltpu.make_async_remote_copy(
            src_ref=sx.at[target],
            dst_ref=sr.at[ctx],
            send_sem=s_s_send,
            recv_sem=s_s_recv,
            device_id=(target, z),
            device_id_type=MESH,
        ).start()
        return carry

    lax.fori_loop(1, n_ctx, send_s, 0)
    sr[ctx] = sx[ctx]


    part = sr.at[0 : n_ctx - 1]
    pltpu.make_async_copy(part, part, s_s_recv).wait()
    near = merged(sr[...])

    adapters_here()
    rank = down_hbm.shape[1]
    width = n_row * rank // 2
    dt[...] = ad[:, :, 0].reshape(n_row * rank, 2 * HD).T
    row = lax.broadcasted_iota(jnp.int32, (2 * OWN, width), 0)
    col = lax.broadcasted_iota(jnp.int32, (2 * OWN, width), 1)
    wanted = jnp.zeros((2 * OWN, width), jnp.int32)
    for k in range(OWN):
        adapter = idx_ref[0, k]
        wanted = jnp.where(
            lax.rem(row, OWN) == k, (adapter % NEAR) * groups + adapter // NEAR, wanted
        )
    mine = wanted == col // rank + (n_row // 2) * (row // OWN)
    seated = col // rank == lax.rem(row, OWN)

    def fold(value):
        shift = width // 2
        while shift >= rank:
            value = value + pltpu.roll(value, shift, 1)
            shift //= 2
        return value


    part = zr.at[0 : n_row - 1]
    pltpu.make_async_copy(part, part, s_z_recv).wait()
    far = merged(zr[...])
    top = jnp.maximum(near[0], far[0])
    parts = [jnp.exp2(near[0] - top), jnp.exp2(far[0] - top)]
    total = parts[0] * near[1] + parts[1] * far[1]
    acc = parts[0] * near[2] + parts[1] * far[2]
    attended = (acc / total).astype(BF16).astype(F32)
    attended = jnp.concatenate([attended[0:OWN], attended[OWN : 2 * OWN]], axis=1)
    out_ref[0] = attended.astype(BF16)

    twice = jnp.concatenate([attended, attended], axis=0).astype(BF16)
    low = jnp.dot(twice, dt[...], preferred_element_type=F32)
    low = jnp.where(row < OWN, low[:, :width], low[:, width:])
    low = fold(jnp.where(mine, low, 0.0))
    ls[...] = jnp.sum(jnp.where(seated, low, 0.0), axis=0, keepdims=True)

    def send_l(d, carry):
        pltpu.make_async_remote_copy(
            src_ref=ls,
            dst_ref=lr.at[ctx],
            send_sem=s_l_send,
            recv_sem=s_l_recv,
            device_id=(lax.rem(ctx + across(d, n_ctx), n_ctx), z),
            device_id_type=MESH,
        ).start()
        return carry

    lax.fori_loop(1, n_ctx, send_l, 0)
    lr[ctx] = ls[...]
    pltpu.make_async_copy(lr.at[0 : n_ctx - 1], lr.at[0 : n_ctx - 1], s_l_recv).wait()
    low = jnp.broadcast_to(jnp.sum(lr[...], axis=0), (2 * OWN, width))
    low = jnp.where(mine, fold(jnp.where(seated, low, 0.0)), 0.0).astype(BF16)
    up = ad[:, :, 1].reshape(n_row * rank, 2 * HD)
    first = jnp.dot(low, up[:width], preferred_element_type=F32)
    second = jnp.dot(low, up[width:], preferred_element_type=F32)
    delta = first[0:OWN] + second[OWN : 2 * OWN]
    out_ref[1] = (attended + delta.astype(BF16).astype(F32)).astype(BF16)

    finish(99)


def body(n_ctx, n_row, queries, prefix, suffix, lengths, adapters, down, up):
    chips = n_ctx // 2
    pairs = chips // 2
    breadth = chips // COLUMN
    lanes = n_row * 8
    pd = prefix.shape[1]
    sd = suffix.shape[1] * suffix.shape[2]
    width = prefix.shape[2]
    rank = down.shape[2]
    suffix = suffix.reshape(2, sd, width)
    adapters = adapters.T
    down = jnp.transpose(down, (0, 2, 1))
    hbm = pl.BlockSpec(memory_space=pltpu.HBM)
    vmem = pl.BlockSpec(memory_space=pltpu.VMEM)
    dma = pltpu.SemaphoreType.DMA
    both = pl.pallas_call(
        functools.partial(kernel, n_ctx, n_row),
        out_shape=jax.ShapeDtypeStruct((2, OWN, 2 * HD), BF16),
        in_specs=[hbm] * 7,
        out_specs=vmem,
        scratch_shapes=[
            pltpu.SMEM(lengths.shape, jnp.int32),
            pltpu.SMEM(adapters.shape, jnp.int32),
            pltpu.VMEM(queries.shape, BF16),
            pltpu.VMEM((pairs * GROUP * OWN, HD), F32),
            pltpu.VMEM((VEC, HD), F32),
            pltpu.VMEM(suffix.shape, BF16),
            pltpu.VMEM((n_ctx, 16, HD), BF16),
            pltpu.VMEM((n_ctx, 16, HD), BF16),
            pltpu.VMEM((2, 2 * breadth, pd, HD), BF16),
            pltpu.VMEM((breadth, HD, 2 * pd), BF16),
            pltpu.VMEM((2, n_row * VEC, HD), BF16),
            pltpu.VMEM((2, breadth, 2 * pd, 2 * lanes), F32),
            pltpu.VMEM((4, HD + EXTRA, lanes), BF16),
            pltpu.VMEM((4, HD + EXTRA, lanes), BF16),
            pltpu.VMEM((n_row, 16, HD), BF16),
            pltpu.VMEM((n_row, 16, HD), BF16),
            pltpu.VMEM((NEAR, n_row // NEAR, 2, rank, 2 * HD), BF16),
            pltpu.VMEM((2 * HD, n_row * rank), BF16),
            pltpu.VMEM((1, n_row * rank // 2), F32),
            pltpu.VMEM((n_ctx, 1, n_row * rank // 2), F32),
            dma,
            dma,
            dma((4,)),
            dma((3,)),
            dma((3,)),
            dma((2,)),
            dma((2, 3)),
            dma,
            dma((2, 2 * breadth)),
            dma,
            dma,
            dma,
            dma,
            dma,
            dma,
            dma,
            dma,
        ],
        compiler_params=pltpu.CompilerParams(
            collective_id=0, has_side_effects=True, vmem_limit_bytes=64 * 1024 * 1024
        ),
        name="decode_attention",
    )(queries, prefix, suffix, lengths, adapters, down, up)
    return both[0], both[1]


def solution(mesh):
    return jax.shard_map(
        functools.partial(body, mesh.shape["ctx"], mesh.shape["row"]),
        mesh=mesh,
        in_specs=(
            P("row", None),
            P(None, ("ctx", "row"), None),
            P(None, "row", "ctx", None),
            P("row"),
            P("row", None),
            P("row", "ctx", None),
            P("row", None, "ctx"),
        ),
        out_specs=(P("row", "ctx"), P("row", "ctx")),
        check_vma=False,
    )
```

```python
import functools
import math

import jax
import jax.numpy as jnp
from jax import lax
from jax.experimental import pallas as pl
from jax.experimental.pallas import tpu as pltpu
from jax.sharding import PartitionSpec as P

HD = 128
GROUP = 8
OWN = 4
VEC = 16
EXTRA = 16
COLUMN = 4
NEAR = 4
MESH = pl.DeviceIdType.MESH
F32 = jnp.float32
BF16 = jnp.bfloat16


def three(value):
    high = value.astype(BF16).astype(F32)
    rest = value - high
    middle = rest.astype(BF16).astype(F32)
    return [high, middle, rest - middle]


def stacked(parts, shape, axis):
    at = lax.broadcasted_iota(jnp.int32, shape, axis)
    out = jnp.zeros(shape, F32)
    for index, part in enumerate(parts):
        out = jnp.where(at == index, jnp.broadcast_to(part, shape), out)
    return out


def contract_last(a, b):
    return lax.dot_general(a, b, (((1,), (1,)), ((), ())), preferred_element_type=F32)


def merged(arrived):
    count = arrived.shape[0]
    wide = arrived.astype(F32)
    extra = wide[:, 8:16, :].reshape(count * 8, HD).astype(BF16)
    row = lax.broadcasted_iota(jnp.int32, (HD, 2 * HD), 0)
    col = lax.broadcasted_iota(jnp.int32, (HD, 2 * HD), 1)
    pick = jnp.where(row // 3 == col // HD, 1.0, 0.0).astype(BF16)
    spread = jnp.dot(extra, pick, preferred_element_type=F32)
    tops = spread[:, :HD].reshape(count, 8, HD)
    totals = spread[:, HD:].reshape(count, 8, HD)
    top = jnp.max(tops, axis=0)
    factor = jnp.exp2(tops - top[None])
    return top, jnp.sum(factor * totals, axis=0), jnp.sum(factor * wide[:, 0:8, :], axis=0)


def kernel(
    n_ctx,
    n_row,
    q_hbm,
    kv_hbm,
    suf_hbm,
    len_hbm,
    idx_hbm,
    down_hbm,
    up_hbm,
    out_ref,
    len_ref,
    idx_ref,
    qv,
    qall,
    qown,
    sufv,
    sx,
    sr,
    kvb,
    vt,
    qb,
    sc,
    ob,
    rb,
    zs,
    zr,
    ad,
    dt,
    ls,
    lr,
    s_q,
    s_suf,
    s_ad_loc,
    s_ad_send,
    s_ad_recv,
    s_a_send,
    s_a_recv,
    s_kv_send,
    s_kv_recv,
    s_s_send,
    s_s_recv,
    s_o_send,
    s_o_recv,
    s_z_send,
    s_z_recv,
    s_l_send,
    s_l_recv,
):
    chips = n_ctx // 2
    pairs = chips // 2
    breadth = chips // COLUMN
    lanes = n_row * 8
    pd = kv_hbm.shape[1]
    sd = suf_hbm.shape[1]
    spos = sd // OWN
    scale = HD**-0.5 * math.log2(math.e)

    ctx = lax.axis_index("ctx")
    z = lax.axis_index("row")
    c = lax.rem(ctx, 2)
    groups = n_row // NEAR
    zl = lax.rem(z, NEAR)
    zh = z // NEAR
    chip = ctx // 2
    x = chip // COLUMN
    y = lax.rem(chip, COLUMN)
    sib = ctx + 1 - 2 * c

    owns = y % 2 == x // 2
    lead = jnp.where(owns, x, (x + 2) % COLUMN)
    g0 = 2 * lead + jnp.where(owns, y, (y + 2) % COLUMN) // 2
    seat = 2 * jnp.where(owns, 0, 1) + c

    def across(i, count):
        return count // 2 + jnp.where(i % 2 == 0, -(i // 2), i // 2)

    barrier = pltpu.get_barrier_semaphore()

    def greet_line(d, carry):
        target = lax.rem(z + d + jnp.where(d < NEAR, n_row - NEAR, n_row - NEAR + 1), n_row)
        for there in (ctx, sib):
            pl.semaphore_signal(barrier, 1, device_id=(there, target), device_id_type=MESH)
        return carry

    def greet_plane(d, carry):
        pl.semaphore_signal(
            barrier,
            1,
            device_id=(lax.rem(ctx + across(d, n_ctx), n_ctx), z),
            device_id_type=MESH,
        )
        return carry

    lax.fori_loop(1, n_ctx, greet_plane, 0)
    lax.fori_loop(0, 2 * NEAR, greet_line, 0)

    q_copy = pltpu.make_async_copy(q_hbm, qv, s_q)
    q_copy.start()
    suf_copy = pltpu.make_async_copy(suf_hbm, sufv, s_suf)
    suf_copy.start()
    ad_loc = [
        pltpu.make_async_copy(down_hbm.at[0], ad.at[zl, zh, 0], s_ad_loc.at[0]),
        pltpu.make_async_copy(up_hbm.at[0], ad.at[zl, zh, 1], s_ad_loc.at[1]),
    ]
    ad_loc.append(pltpu.make_async_copy(len_hbm, len_ref, s_ad_loc.at[2]))
    ad_loc.append(pltpu.make_async_copy(idx_hbm, idx_ref, s_ad_loc.at[3]))
    for copy in ad_loc:
        copy.start()

    q_copy.wait()
    queries = qv[...].astype(F32)
    for head in range(pairs * GROUP):
        qall[head * OWN : (head + 1) * OWN, :] = queries[:, head * HD : (head + 1) * HD]
    for side in range(2):
        start = pl.multiple_of(g0 * (GROUP * OWN) + side * VEC + 8 * c, 8)
        qown[side * 8 : (side + 1) * 8, :] = qall[pl.ds(start, 8), :]
    qb[c, 0:VEC, :] = qown[...].astype(BF16)

    pl.semaphore_wait(barrier, n_ctx - 1 + 4 * NEAR)

    def send_q(first, count, place, there, step, sems):
        pltpu.make_async_remote_copy(
            src_ref=qb.at[c, first * VEC : (first + count) * VEC],
            dst_ref=qb.at[c, place * VEC : (place + count) * VEC],
            send_sem=s_a_send.at[sems // 2],
            recv_sem=s_a_recv.at[c, sems],
            device_id=(there, lax.rem(z + step + n_row, n_row)),
            device_id_type=MESH,
        ).start()

    def wait_q(core, kind, count):
        part = qb.at[0, 0 : count * VEC]
        pltpu.make_async_copy(part, part, s_a_recv.at[core, kind]).wait()

    for d in range(NEAR, 0, -1):
        for there in (ctx, sib):
            send_q(0, 1, n_row - d, there, d, 0)
        if d < NEAR:
            for there in (ctx, sib):
                send_q(0, 1, d, there, -d, 1)
    send_q(0, 1, 0, sib, 0, 1)

    def send_far(block, step, kind):
        pltpu.make_async_remote_copy(
            src_ref=ad.at[zl, block],
            dst_ref=ad.at[zl, block],
            send_sem=s_ad_send.at[kind],
            recv_sem=s_ad_recv.at[kind],
            device_id=(ctx, lax.rem(z + step + n_row, n_row)),
            device_id_type=MESH,
        ).start()

    def pass_adapters():
        part = ad.at[0, 0:2]
        pltpu.make_async_copy(part, part, s_ad_recv.at[0]).wait()
        send_far(lax.rem(zh + groups - 1, groups), NEAR, 1)

    def share_adapters():
        part = ad.at[0, 0]
        pltpu.make_async_copy(part, part, s_ad_recv.at[1]).wait()
        for d in (1, n_row - 1, 2):
            pltpu.make_async_remote_copy(
                src_ref=ad.at[zl],
                dst_ref=ad.at[zl],
                send_sem=s_ad_send.at[2],
                recv_sem=s_ad_recv.at[2],
                device_id=(ctx, lax.rem(z + d, n_row)),
                device_id_type=MESH,
            ).start()

    for copy in ad_loc:
        copy.wait()
    send_far(zh, NEAR, 0)
    send_far(zh, -NEAR, 0)

    def place_kv(i, g):
        home_x = g // 2
        home_y = 2 * (g % 2) + g // 4
        dx = (x - home_x + COLUMN) % COLUMN
        dy = (y - home_y + COLUMN) % COLUMN
        far = jnp.where(dx == 3, 1, dx) + jnp.where(dy == 3, 1, dy)
        level = jnp.where(dx == dy, 1, jnp.where(dx == 2 * (g % 2), 1, 0))
        level = jnp.where(jnp.logical_and(dx % 2 == 1, dx != dy), 0, level)
        stay = jnp.where(far == 2, level, jnp.where(far < 2, 1, 0))
        dx = (dx + 2 * (1 - stay)) % COLUMN
        dy = (dy + 2 * (1 - stay)) % COLUMN
        target_x = (home_x + 2 * (1 - stay)) % COLUMN
        target_y = (home_y + 2 * (1 - stay)) % COLUMN
        one = jnp.where(dy == 0, (dx + 1) // 2, jnp.where(dy == 1, 3, 4))
        two = jnp.where(dx % 2 == 1, 5 + dx // 2, 7)
        near = jnp.logical_or(dx % 2 == 0, dy % 2 == 0)
        near = jnp.logical_and(near, jnp.logical_and(dx != 2, dy != 2))
        slot = jnp.where(near, one, two)
        columns = pl.ds(pl.multiple_of(g * HD, HD), HD)
        return target_x * COLUMN + target_y, slot, kv_hbm.at[i, :, columns]

    def send_cache(i):
        def send_kv(d, carry):
            target, slot, part = place_kv(i, lax.rem(g0 + d, pairs))
            pltpu.make_async_remote_copy(
                src_ref=part,
                dst_ref=kvb.at[i, slot],
                send_sem=s_kv_send,
                recv_sem=s_kv_recv.at[i, slot],
                device_id=(target * 2 + c, z),
                device_id_type=MESH,
            ).start()
            return carry

        lax.fori_loop(1, pairs, send_kv, 0)
        _, slot, part = place_kv(i, g0)
        pltpu.make_async_copy(part, kvb.at[i, slot], s_kv_recv.at[i, slot]).start()

    send_cache(0)

    wait_q(c, 0, NEAR)
    for there in (ctx, sib):
        send_q(n_row - NEAR, NEAR, n_row - 2 * NEAR, there, NEAR, 2)
    wait_q(c, 1, NEAR - 1)
    for there in (ctx, sib):
        send_q(0, NEAR, NEAR, there, -NEAR, 2)

    send_cache(1)
    pass_adapters()

    suf_copy.wait()
    at = lax.broadcasted_iota(jnp.int32, (GROUP * OWN, sd), 1)
    row = lax.broadcasted_iota(jnp.int32, (GROUP * OWN, sd), 0)
    owner = at // spos
    live = jnp.zeros((GROUP * OWN, sd), jnp.int32)
    for k in range(OWN):
        live = jnp.where(owner == k, len_ref[k], live)
    valid = (lax.rem(row, OWN) == owner) & (ctx * spos + lax.rem(at, spos) < live)
    for g in range(pairs):
        vectors = qall[g * GROUP * OWN : (g + 1) * GROUP * OWN, :].astype(BF16)
        scores = contract_last(vectors, sufv[0, :, g * HD : (g + 1) * HD]) * scale
        scores = jnp.where(valid, scores, -1e30)
        top = jnp.max(scores, axis=1, keepdims=True)
        weights = jnp.exp2(scores - top)
        total = jnp.sum(weights, axis=1, keepdims=True)
        out = jnp.dot(
            weights.astype(BF16),
            sufv[1, :, g * HD : (g + 1) * HD],
            preferred_element_type=F32,
        )
        extra = stacked(three(top) + three(total), (GROUP * OWN, HD), 1)
        sx[4 * g : 4 * g + 4] = jnp.concatenate(
            [out.reshape(4, 8, HD), extra.reshape(4, 8, HD)], axis=1
        ).astype(BF16)

    def adapters_here():
        part = ad.at[0 : NEAR - 1]
        pltpu.make_async_copy(part, part, s_ad_recv.at[2]).wait()

    def finish(k):
        part = ad.at[0, 0:2]
        pltpu.make_async_copy(part, part, s_ad_send.at[0]).wait()
        part = ad.at[0, 0]
        pltpu.make_async_copy(part, part, s_ad_send.at[1]).wait()
        part = ad.at[0 : NEAR - 1]
        pltpu.make_async_copy(part, part, s_ad_send.at[2]).wait()
        part = qb.at[0, 0 : (4 * NEAR - 1) * VEC]
        pltpu.make_async_copy(part, part, s_a_send.at[0]).wait()
        part = qb.at[0, 0 : 4 * NEAR * VEC]
        pltpu.make_async_copy(part, part, s_a_send.at[1]).wait()
        part = kvb.at[:, 0 : pairs - 1]
        pltpu.make_async_copy(part, part, s_kv_send).wait()
        part = sx.at[0 : n_ctx - 1]
        pltpu.make_async_copy(part, part, s_s_send).wait()
        part = ob.at[0:3]

        @pl.when(owns)
        def _():
            pltpu.make_async_copy(part, part, s_o_send).wait()

        @pl.when(jnp.logical_not(owns))
        def _():
            pltpu.make_async_copy(ob, ob, s_o_send).wait()

        part = zs.at[0 : n_row - 1]
        pltpu.make_async_copy(part, part, s_z_send).wait()
        part = lr.at[0 : n_ctx - 1]
        pltpu.make_async_copy(part, part, s_l_send).wait()

    wait_q(c, 2, 2 * NEAR)

    def vectors_of(core):
        wide = qb[core].astype(F32).reshape(n_row, 2, 8, HD)
        return jnp.concatenate(
            [wide[:, side].reshape(lanes, HD) for side in range(2)], axis=0
        ).astype(BF16)

    def arrive(i, j):
        for side in range(2):
            slot = 2 * j + side
            pltpu.make_async_copy(
                kvb.at[i, slot], kvb.at[i, slot], s_kv_recv.at[i, slot]
            ).wait()

    cores = (c, 1 - c)
    for h in range(2):
        if h == 1:
            wait_q(1 - c, 0, NEAR)
            wait_q(1 - c, 1, NEAR)
            wait_q(1 - c, 2, 2 * NEAR)
        vectors = vectors_of(cores[h])
        top = None
        for j in range(breadth):
            if h == 0:
                arrive(0, j)
            keys = kvb[0, 2 * j : 2 * j + 2].reshape(2 * pd, HD)
            scores = contract_last(keys, vectors) * scale
            sc[h, j] = scores
            best = jnp.max(scores, axis=0, keepdims=True)
            top = best if top is None else jnp.maximum(top, best)
        total = jnp.zeros((1, 2 * lanes), F32)
        acc = jnp.zeros((HD, 2 * lanes), F32)
        for j in range(breadth):
            if h == 0:
                arrive(1, j)
                vt[j] = kvb[1, 2 * j : 2 * j + 2].reshape(2 * pd, HD).T
            weights = jnp.exp2(sc[h, j] - top)
            total = total + jnp.sum(weights, axis=0, keepdims=True)
            acc = acc + jnp.dot(vt[j], weights.astype(BF16), preferred_element_type=F32)
        extra = stacked(three(top) + three(total), (EXTRA, 2 * lanes), 0)
        for side in range(2):
            target = (g0 * 2 + side) * 2 + cores[h]
            index = 2 * side + cores[h]
            columns = slice(side * lanes, (side + 1) * lanes)
            ob[index, 0:HD, :] = acc[:, columns].astype(BF16)
            ob[index, HD : HD + EXTRA, :] = extra[:, columns].astype(BF16)

            @pl.when(target != ctx)
            def _():
                pltpu.make_async_remote_copy(
                    src_ref=ob.at[index],
                    dst_ref=rb.at[seat],
                    send_sem=s_o_send,
                    recv_sem=s_o_recv,
                    device_id=(target, z),
                    device_id_type=MESH,
                ).start()

            @pl.when(target == ctx)
            def _():
                pltpu.make_async_copy(ob.at[index], rb.at[seat], s_o_recv).start()

    share_adapters()

    pltpu.make_async_copy(rb, rb, s_o_recv).wait()
    tops, totals = [], []
    for k in range(4):
        extra = rb[k, HD : HD + EXTRA, :].astype(F32)
        tops.append(extra[0:1] + extra[1:2] + extra[2:3])
        totals.append(extra[3:4] + extra[4:5] + extra[5:6])
    top = functools.reduce(jnp.maximum, tops)
    acc = jnp.zeros((HD, lanes), F32)
    total = jnp.zeros((1, lanes), F32)
    for k in range(4):
        factor = jnp.exp2(tops[k] - top)
        acc = acc + factor * rb[k, 0:HD, :].astype(F32)
        total = total + factor * totals[k]
    extra = stacked(three(top) + three(total), (HD, lanes), 0)
    zs[...] = jnp.concatenate(
        [acc.T.reshape(n_row, 8, HD), extra.T.reshape(n_row, 8, HD)], axis=1
    ).astype(BF16)

    def send_z(i, carry):
        target = i - 1 + jnp.where(i > z, 1, 0)
        step = lax.rem(target - z + n_row, n_row)
        pltpu.make_async_remote_copy(
            src_ref=zs.at[step],
            dst_ref=zr.at[z],
            send_sem=s_z_send,
            recv_sem=s_z_recv,
            device_id=(ctx, target),
            device_id_type=MESH,
        ).start()
        return carry

    lax.fori_loop(1, n_row, send_z, 0)
    zr[z] = zs[0]
    def send_s(d, carry):
        target = lax.rem(ctx + d, n_ctx)
        pltpu.make_async_remote_copy(
            src_ref=sx.at[target],
            dst_ref=sr.at[ctx],
            send_sem=s_s_send,
            recv_sem=s_s_recv,
            device_id=(target, z),
            device_id_type=MESH,
        ).start()
        return carry

    lax.fori_loop(1, n_ctx, send_s, 0)
    sr[ctx] = sx[ctx]


    part = sr.at[0 : n_ctx - 1]
    pltpu.make_async_copy(part, part, s_s_recv).wait()
    near = merged(sr[...])

    adapters_here()
    rank = down_hbm.shape[1]
    width = n_row * rank // 2
    dt[...] = ad[:, :, 0].reshape(n_row * rank, 2 * HD).T
    row = lax.broadcasted_iota(jnp.int32, (2 * OWN, width), 0)
    col = lax.broadcasted_iota(jnp.int32, (2 * OWN, width), 1)
    wanted = jnp.zeros((2 * OWN, width), jnp.int32)
    for k in range(OWN):
        adapter = idx_ref[0, k]
        wanted = jnp.where(
            lax.rem(row, OWN) == k, (adapter % NEAR) * groups + adapter // NEAR, wanted
        )
    mine = wanted == col // rank + (n_row // 2) * (row // OWN)
    seated = col // rank == lax.rem(row, OWN)

    def fold(value):
        shift = width // 2
        while shift >= rank:
            value = value + pltpu.roll(value, shift, 1)
            shift //= 2
        return value


    part = zr.at[0 : n_row - 1]
    pltpu.make_async_copy(part, part, s_z_recv).wait()
    far = merged(zr[...])
    top = jnp.maximum(near[0], far[0])
    parts = [jnp.exp2(near[0] - top), jnp.exp2(far[0] - top)]
    total = parts[0] * near[1] + parts[1] * far[1]
    acc = parts[0] * near[2] + parts[1] * far[2]
    attended = (acc / total).astype(BF16).astype(F32)
    attended = jnp.concatenate([attended[0:OWN], attended[OWN : 2 * OWN]], axis=1)
    out_ref[0] = attended.astype(BF16)

    twice = jnp.concatenate([attended, attended], axis=0).astype(BF16)
    low = jnp.dot(twice, dt[...], preferred_element_type=F32)
    low = jnp.where(row < OWN, low[:, :width], low[:, width:])
    low = fold(jnp.where(mine, low, 0.0))
    ls[...] = jnp.sum(jnp.where(seated, low, 0.0), axis=0, keepdims=True)

    def send_l(d, carry):
        pltpu.make_async_remote_copy(
            src_ref=ls,
            dst_ref=lr.at[ctx],
            send_sem=s_l_send,
            recv_sem=s_l_recv,
            device_id=(lax.rem(ctx + across(d, n_ctx), n_ctx), z),
            device_id_type=MESH,
        ).start()
        return carry

    lax.fori_loop(1, n_ctx, send_l, 0)
    lr[ctx] = ls[...]
    pltpu.make_async_copy(lr.at[0 : n_ctx - 1], lr.at[0 : n_ctx - 1], s_l_recv).wait()
    low = jnp.broadcast_to(jnp.sum(lr[...], axis=0), (2 * OWN, width))
    low = jnp.where(mine, fold(jnp.where(seated, low, 0.0)), 0.0).astype(BF16)
    up = ad[:, :, 1].reshape(n_row * rank, 2 * HD)
    first = jnp.dot(low, up[:width], preferred_element_type=F32)
    second = jnp.dot(low, up[width:], preferred_element_type=F32)
    delta = first[0:OWN] + second[OWN : 2 * OWN]
    out_ref[1] = (attended + delta.astype(BF16).astype(F32)).astype(BF16)

    finish(99)


def body(n_ctx, n_row, queries, prefix, suffix, lengths, adapters, down, up):
    chips = n_ctx // 2
    pairs = chips // 2
    breadth = chips // COLUMN
    lanes = n_row * 8
    pd = prefix.shape[1]
    sd = suffix.shape[1] * suffix.shape[2]
    width = prefix.shape[2]
    rank = down.shape[2]
    suffix = suffix.reshape(2, sd, width)
    adapters = adapters.T
    down = jnp.transpose(down, (0, 2, 1))
    hbm = pl.BlockSpec(memory_space=pltpu.HBM)
    vmem = pl.BlockSpec(memory_space=pltpu.VMEM)
    dma = pltpu.SemaphoreType.DMA
    both = pl.pallas_call(
        functools.partial(kernel, n_ctx, n_row),
        out_shape=jax.ShapeDtypeStruct((2, OWN, 2 * HD), BF16),
        in_specs=[hbm] * 7,
        out_specs=vmem,
        scratch_shapes=[
            pltpu.SMEM(lengths.shape, jnp.int32),
            pltpu.SMEM(adapters.shape, jnp.int32),
            pltpu.VMEM(queries.shape, BF16),
            pltpu.VMEM((pairs * GROUP * OWN, HD), F32),
            pltpu.VMEM((VEC, HD), F32),
            pltpu.VMEM(suffix.shape, BF16),
            pltpu.VMEM((n_ctx, 16, HD), BF16),
            pltpu.VMEM((n_ctx, 16, HD), BF16),
            pltpu.VMEM((2, 2 * breadth, pd, HD), BF16),
            pltpu.VMEM((breadth, HD, 2 * pd), BF16),
            pltpu.VMEM((2, n_row * VEC, HD), BF16),
            pltpu.VMEM((2, breadth, 2 * pd, 2 * lanes), F32),
            pltpu.VMEM((4, HD + EXTRA, lanes), BF16),
            pltpu.VMEM((4, HD + EXTRA, lanes), BF16),
            pltpu.VMEM((n_row, 16, HD), BF16),
            pltpu.VMEM((n_row, 16, HD), BF16),
            pltpu.VMEM((NEAR, n_row // NEAR, 2, rank, 2 * HD), BF16),
            pltpu.VMEM((2 * HD, n_row * rank), BF16),
            pltpu.VMEM((1, n_row * rank // 2), F32),
            pltpu.VMEM((n_ctx, 1, n_row * rank // 2), F32),
            dma,
            dma,
            dma((4,)),
            dma((3,)),
            dma((3,)),
            dma((2,)),
            dma((2, 3)),
            dma,
            dma((2, 2 * breadth)),
            dma,
            dma,
            dma,
            dma,
            dma,
            dma,
            dma,
            dma,
        ],
        compiler_params=pltpu.CompilerParams(
            collective_id=0, has_side_effects=True, vmem_limit_bytes=64 * 1024 * 1024
        ),
        name="decode_attention",
    )(queries, prefix, suffix, lengths, adapters, down, up)
    return both[0], both[1]


def solution(mesh):
    return jax.shard_map(
        functools.partial(body, mesh.shape["ctx"], mesh.shape["row"]),
        mesh=mesh,
        in_specs=(
            P("row", None),
            P(None, ("ctx", "row"), None),
            P(None, "row", "ctx", None),
            P("row"),
            P("row", None),
            P("row", "ctx", None),
            P("row", None, "ctx"),
        ),
        out_specs=(P("row", "ctx"), P("row", "ctx")),
        check_vma=False,
    )
```
